32 devices in a mesh: groups: 2 (over y), lat: 4 (over z), chan: 4 (over x, core).
Axes of the slice: x: 2, y: 2, z: 4, core: 2. Of those that a mesh axis runs over, the one named last changes fastest.
Arguments:
- grid_input: bfloat16 [16, 1440, 1024], P(('groups', 'lat'), None, 'chan'), parts along dimension 0, may hold values from -6 to 6
- legendre: bfloat16 [64, 512, 8], P(('lat', 'chan')), may hold values from -2 to 2
- mix_weight: bfloat16 [1024, 1024], P(None, 'lat'), may hold values from -0.1875 to 0.1875
- degree_gain: float32 [512], replicated, may hold values from 0.3 to 3
- order_slot: int32 [64], replicated, may hold values from 0 to 63, as said below
Outputs:
- grid_output: bfloat16 [16, 1440, 1024], P(('groups', 'lat'), None, 'chan'), parts along dimension 0
The draws below stay inside these ranges and needn't reach their ends.
There are 2 independent parts, one for each index of `groups`. The reference program is written for one: setup_inputs(seed, part) draws one part's arguments, and reference() takes and returns one part's arrays. A program takes and returns all parts, laid end to end along the dimension named above; an argument that names none is the same for every part. Nothing has to cross between parts.
Inputs may be any that keep to these rules, and one draw needn't show every extreme that they name: order_slot is a permutation of the orders 0 to 63.
All inputs are finite; a program needn't handle non-finite values.
Results may differ from the reference program's by a relative error of at most 0.0067.
Values may be sent and summed in bfloat16 or wider, within the bound.
No kernel may reach another device: no remote copies, remote signals or barrier semaphores. Data moves between devices by JAX's collectives and lax.ppermute only.
A program may use at most 64 MiB of HBM per device.

```python
import math
import jax
import jax.numpy as jnp
from jax import lax

C = 1024
NLON = 1440
LDEG = 512
ORD_DEV = 16
ORDERS = 64
NLAT = 8


def draw_order_slot(key, part):
    key = jax.random.fold_in(key, 11)
    return jax.random.permutation(key, jnp.arange(ORDERS, dtype=jnp.int32)).astype(jnp.int32)


def level_of(key, dims, split, least, high):
    level, own = 1.0, jax.random.fold_in(key, 6)
    for axis_at, shards_of in split:
        heights = jnp.exp(jax.random.uniform(jax.random.fold_in(own, axis_at), (shards_of,), jnp.float32, least / len(split), high / len(split)))
        level = level * jnp.repeat(heights, dims[axis_at] // shards_of).reshape([-1 if axis == axis_at else 1 for axis in range(len(dims))])
    return level


def gaussian(rng, shape, deviation, most, pieces=(), kind=jnp.bfloat16):
    result = deviation * jax.random.normal(rng, shape, jnp.float32)
    if pieces:
        result = result * level_of(rng, shape, pieces, -0.22, 0.18)
    return jnp.clip(result, -most, most).astype(kind)


def setup_inputs(seed: int = 0, part: int = 0) -> dict:
    streams_of = jax.random.split(jax.random.key(seed), 6)
    own_keys = jax.random.split(jax.random.fold_in(streams_of[5], part), 6)
    grid_input = gaussian(own_keys[0], (NLAT, NLON, C), 1.0, 6.0, ((0, 4), (2, 4)))
    legendre = gaussian(streams_of[1], (ORDERS, LDEG, NLAT), NLAT ** -0.5, 2.0, ((0, 16),))
    mix_weight = gaussian(streams_of[2], (C, C), C ** -0.5, 0.1875, ((1, 4),))
    degree_gain = jnp.clip(jnp.exp(jax.random.uniform(streams_of[3], (LDEG,), jnp.float32, math.log(0.3), math.log(3.0))), 0.3, 3.0)
    order_slot = draw_order_slot(jax.random.fold_in(streams_of[5], 71), part)
    return dict(grid_input=grid_input, legendre=legendre, mix_weight=mix_weight, degree_gain=degree_gain, order_slot=order_slot)


def transform_tables(order_index, longitudes):
    steps_along = jnp.arange(longitudes, dtype=jnp.int32)
    residue = steps_along[:, None] * order_index[None, :] % longitudes
    angle_value = residue.astype(jnp.float32) * (2.0 * math.pi / longitudes)
    factor = 1.0 / math.sqrt(longitudes)
    weight = jnp.where(order_index == 0, 1.0, 2.0).astype(jnp.float32)
    cosine = jnp.cos(angle_value) * factor
    sine_part = jnp.sin(angle_value) * factor
    forward_table = jnp.concatenate([cosine, -sine_part], axis=1).astype(jnp.bfloat16)
    inverse_table = jnp.concatenate([weight[None, :] * cosine, -weight[None, :] * sine_part], axis=1).astype(jnp.bfloat16)
    return (forward_table, inverse_table)

def reference(grid_input, legendre, mix_weight, degree_gain, order_slot):
    forward_table, inverse_table = transform_tables(order_slot, NLON)
    spectrum = jnp.einsum('akc,kn->anc', grid_input.astype(jnp.float32), forward_table.astype(jnp.float32))
    spectrum = spectrum.reshape(NLAT, 2, ORDERS, C).astype(jnp.bfloat16)
    block_count = ORDERS // ORD_DEV
    grouped = spectrum.reshape(NLAT, 2, block_count, ORD_DEV, C).transpose(2, 0, 1, 3, 4)
    tables = legendre.reshape(block_count, ORD_DEV, LDEG, NLAT)
    firsts = (order_slot // 64).astype(jnp.int32).reshape(block_count, ORD_DEV)
    factor = math.sqrt(NLAT / LDEG)
    weights = mix_weight.astype(jnp.float32)
    gain_values = degree_gain.astype(jnp.float32)
    degree_block = jnp.arange(LDEG, dtype=jnp.int32) // 64

    def one_block(operands):
        rows_here, table_block, first_rows = operands
        table_wide = table_block.astype(jnp.float32)
        coefficients = jnp.einsum('slt,trsc->slrc', table_wide, rows_here.astype(jnp.float32))
        alive_mask = degree_block[None, :] >= first_rows[:, None]
        coefficients = jnp.where(alive_mask[:, :, None, None], coefficients, 0.0).astype(jnp.bfloat16)
        mixed_coef = jnp.einsum('slrc,cd->slrd', coefficients.astype(jnp.float32), weights) * gain_values[None, :, None, None]
        mixed_coef = mixed_coef.astype(jnp.bfloat16)
        synthesis = jnp.einsum('slt,slrd->trsd', table_wide, mixed_coef.astype(jnp.float32)) * factor
        return synthesis.astype(jnp.bfloat16)
    synthesis = lax.map(one_block, (grouped, tables, firsts))
    synthesis = synthesis.transpose(1, 2, 0, 3, 4).reshape(NLAT, 2 * ORDERS, C)
    field_sum = jnp.einsum('anc,kn->akc', synthesis.astype(jnp.float32), inverse_table.astype(jnp.float32))
    return (grid_input.astype(jnp.float32) + jax.nn.gelu(field_sum)).astype(jnp.bfloat16)
```

```python
import functools
import math

import jax
import jax.numpy as jnp
import numpy as np
from jax import lax
from jax.experimental import pallas as pl
from jax.experimental.pallas import tpu as pltpu
from jax.sharding import PartitionSpec as P

LATITUDE_ROWS = 16


def transform_table(orders, longitudes):
    residue = np.arange(longitudes)[:, None] * np.arange(orders)[None, :] % longitudes
    angle = residue.astype(np.float32) * np.float32(2.0 * math.pi / longitudes)
    scale = np.float32(1.0 / math.sqrt(longitudes))
    return np.concatenate([np.cos(angle) * scale, -np.sin(angle) * scale], axis=1).astype(jnp.bfloat16)


def slot_of_row(lat_count, chan_count, slot_count):
    slots = np.arange(lat_count * chan_count * slot_count).reshape(lat_count, chan_count, slot_count)
    groups = slots.transpose(1, 0, 2).reshape(chan_count, 1, -1)
    return np.broadcast_to(groups, (chan_count, 2, groups.shape[2])).reshape(-1)


def place_matrix(lat_count, chan_count, slot_count):
    slots = slot_of_row(lat_count, chan_count, slot_count)
    orders = lat_count * chan_count * slot_count
    part = np.arange(2 * orders) // (orders // chan_count) % 2
    hit = np.arange(orders)[:, None] == slots[None, :]
    return np.stack([hit & (part == 0), hit & (part == 1)]).astype(jnp.bfloat16)


def order_rows(order_ref, place_ref, weighted):
    orders = order_ref.shape[1]
    natural = lax.broadcasted_iota(jnp.int32, (orders, orders), 0)
    value = jnp.where(natural == 0, 1.0, 2.0) if weighted else 1.0
    held = jnp.where(natural == order_ref[...], value, 0.0).astype(jnp.bfloat16)
    halves = [jnp.dot(held, place_ref[r], preferred_element_type=jnp.float32) for r in range(2)]
    return jnp.concatenate(halves, axis=0).astype(jnp.bfloat16)


def analysis_kernel(factor, grid_ref, table_ref, order_ref, place_ref, legendre_ref, gain_ref, slot_ref, rows_ref, pair_ref):
    chan_count, _, group_rows, channels = rows_ref.shape
    spectrum = jnp.dot(table_ref[...], grid_ref[0], preferred_element_type=jnp.float32)
    rows = lax.dot_general(
        order_rows(order_ref, place_ref, False),
        spectrum.astype(jnp.bfloat16),
        (((0,), (0,)), ((), ())),
        preferred_element_type=jnp.float32,
    )
    rows_ref[:, 0] = rows.astype(jnp.bfloat16).reshape(chan_count, group_rows, channels)

    @pl.when(pl.program_id(0) == 0)
    def _():
        slot_count, latitudes, degrees = legendre_ref.shape
        own = (lax.axis_index("lat") * lax.axis_size("chan") + lax.axis_index("chan")) * slot_count
        block = lax.broadcasted_iota(jnp.int32, (latitudes, degrees), 1) // 64
        pieces = []
        for s in range(slot_count):
            alive = block >= slot_ref[own + s] // 64
            degree_rows = legendre_ref[s].astype(jnp.float32)
            pair = lax.dot_general(
                jnp.where(alive, degree_rows * (gain_ref[...] * factor), 0.0),
                degree_rows,
                (((1,), (1,)), ((), ())),
                precision=lax.Precision.HIGHEST,
                preferred_element_type=jnp.float32,
            )
            high = pair.astype(jnp.bfloat16)
            pieces += [high.astype(jnp.float32), pair - high.astype(jnp.float32)]
        pairs = jnp.concatenate(pieces, axis=1)
        spare = pair_ref.shape[0] - latitudes
        if spare:
            pairs = jnp.concatenate([pairs, jnp.zeros((spare, pairs.shape[1]), jnp.float32)], axis=0)
        pair_ref[...] = pairs.astype(jnp.bfloat16)


def mixing_matrices(lat_count, lat_dev, slots_here, slot_count):
    latitudes = lat_count * lat_dev
    row = np.arange(latitudes * 2 * slots_here)
    t, r, s = row // (2 * slots_here), row // slots_here % 2, row % slots_here
    owner, place = s // slot_count, s % slot_count
    lane = np.arange(slot_count * 2 * latitudes)
    lane_place, lane_t = lane // (2 * latitudes), lane % latitudes
    take = np.arange(lat_count * LATITUDE_ROWS)[None, :] == (owner * LATITUDE_ROWS + t)[:, None]
    own = place[:, None] == lane_place[None, :]
    spread = lane_t[:, None] == t[None, :]
    same = (s[:, None] == s[None, :]) & (r[:, None] == r[None, :])
    return [m.astype(jnp.bfloat16) for m in (take, own, spread, same)]


def mixing_kernel(rows_ref, pair_ref, weight_ref, take_ref, own_ref, spread_ref, same_ref, mixed_ref):
    lat_count, chan_count, part_rows, channels = rows_ref.shape
    count = lat_count * part_rows
    mixed = jnp.zeros((count, weight_ref.shape[1]), jnp.float32)
    for b in range(chan_count):
        mixed = mixed + jnp.dot(
            rows_ref[:, b].reshape(count, channels),
            weight_ref[b * channels : (b + 1) * channels, :],
            preferred_element_type=jnp.float32,
        )
    pairs = pair_ref[...].reshape(lat_count * pair_ref.shape[1], pair_ref.shape[2])
    taken = jnp.dot(take_ref[...], pairs, preferred_element_type=jnp.float32) * own_ref[...].astype(jnp.float32)
    matrix = jnp.dot(taken.astype(jnp.bfloat16), spread_ref[...], preferred_element_type=jnp.float32)
    matrix = matrix * same_ref[...].astype(jnp.float32)
    synthesis = jnp.dot(matrix, mixed, precision=lax.Precision.HIGHEST, preferred_element_type=jnp.float32)
    mixed_ref[...] = synthesis.astype(jnp.bfloat16).reshape(mixed_ref.shape)


def mixing_plain(rows, pairs, weight, lat_dev, slots_here, slot_count):
    lat_count, chan_count, _, channels = rows.shape
    latitudes = lat_count * lat_dev
    wide = pairs[:, :latitudes].astype(jnp.float32).reshape(lat_count, latitudes, slot_count, 2, latitudes)
    matrix = wide.sum(axis=3).transpose(0, 2, 1, 3).reshape(slots_here, latitudes, latitudes)
    mixed = jnp.einsum(
        "abnc,bcd->and", rows, weight.reshape(chan_count, channels, -1), preferred_element_type=jnp.float32
    ).reshape(latitudes, 2, slots_here, -1)
    synthesis = jnp.einsum(
        "svt,trsd->vrsd", matrix, mixed, precision=lax.Precision.HIGHEST, preferred_element_type=jnp.float32
    )
    return synthesis.astype(jnp.bfloat16).reshape(lat_count, lat_dev * 2 * slots_here, -1)


def synthesis_kernel(rows_ref, grid_ref, table_ref, order_ref, place_ref, out_ref):
    chan_count, _, group_rows, channels = rows_ref.shape
    rows = rows_ref[...].reshape(chan_count * group_rows, channels)
    natural = jnp.dot(order_rows(order_ref, place_ref, True), rows, preferred_element_type=jnp.float32)
    field = jnp.dot(table_ref[...], natural.astype(jnp.bfloat16), preferred_element_type=jnp.float32)
    inner = math.sqrt(2.0 / math.pi) * (field + 0.044715 * (field * field * field))
    out_ref[0] = (grid_ref[0].astype(jnp.float32) + 0.5 * field * (1.0 + jnp.tanh(inner))).astype(jnp.bfloat16)


def shards(grid_input, legendre, mix_weight, degree_gain, order_slot):
    lat_dev, longitudes, chan_dev = grid_input.shape
    orders = order_slot.shape[0]
    slot_count, degrees, latitudes = legendre.shape
    lat_count = lax.axis_size("lat")
    chan_count = lax.axis_size("chan")
    slots_here = lat_count * slot_count
    group_rows = 2 * slots_here
    pair_rows = max(latitudes, LATITUDE_ROWS)
    pair_lanes = slot_count * 2 * latitudes
    params = pltpu.CompilerParams(vmem_limit_bytes=40 * 1024 * 1024)

    table = transform_table(orders, longitudes)
    place = jnp.asarray(place_matrix(lat_count, chan_count, slot_count))
    order_row = order_slot.reshape(1, orders)
    whole = lambda shape: pl.BlockSpec(shape, lambda *_: (0,) * len(shape))

    rows, pairs = pl.pallas_call(
        functools.partial(analysis_kernel, math.sqrt(latitudes / degrees)),
        grid=(lat_dev,),
        in_specs=[
            pl.BlockSpec((1, longitudes, chan_dev), lambda t: (t, 0, 0)),
            whole((2 * orders, longitudes)),
            whole((1, orders)),
            whole(place.shape),
            whole((slot_count, latitudes, degrees)),
            whole((1, degrees)),
            pl.BlockSpec(memory_space=pltpu.SMEM),
        ],
        out_specs=[
            pl.BlockSpec((chan_count, 1, group_rows, chan_dev), lambda t: (0, t, 0, 0)),
            whole((pair_rows, pair_lanes)),
        ],
        out_shape=[
            jax.ShapeDtypeStruct((chan_count, lat_dev, group_rows, chan_dev), jnp.bfloat16),
            jax.ShapeDtypeStruct((pair_rows, pair_lanes), jnp.bfloat16),
        ],
        compiler_params=params,
    )(
        grid_input,
        jnp.asarray(np.ascontiguousarray(table.T)),
        order_row,
        place,
        jnp.swapaxes(legendre, 1, 2),
        degree_gain.reshape(1, degrees),
        order_slot,
    )

    rows = rows.reshape(chan_count, lat_dev * group_rows, chan_dev)
    rows = lax.all_to_all(rows, "chan", split_axis=0, concat_axis=0, tiled=True)
    rows, pairs = lax.all_gather((rows, pairs), "lat", axis=0, tiled=False)

    count = latitudes * group_rows
    if count <= 512 and latitudes <= LATITUDE_ROWS:
        helpers = [jnp.asarray(m) for m in mixing_matrices(lat_count, lat_dev, slots_here, slot_count)]
        mixed = pl.pallas_call(
            mixing_kernel,
            out_shape=jax.ShapeDtypeStruct((lat_count, lat_dev * group_rows, mix_weight.shape[1]), jnp.bfloat16),
            compiler_params=params,
        )(rows, pairs, mix_weight, *helpers)
    else:
        mixed = mixing_plain(rows, pairs, mix_weight, lat_dev, slots_here, slot_count)

    back = lax.all_to_all(mixed, "lat", split_axis=0, concat_axis=0, tiled=True)
    if mix_weight.shape[1] != chan_dev:
        back = back.transpose(1, 0, 2).reshape(lat_dev * group_rows, chan_count, chan_dev).transpose(1, 0, 2)
    back = lax.all_to_all(back, "chan", split_axis=0, concat_axis=0, tiled=True)
    back = back.reshape(chan_count, lat_dev, group_rows, chan_dev)

    return pl.pallas_call(
        synthesis_kernel,
        grid=(lat_dev,),
        in_specs=[
            pl.BlockSpec((chan_count, 1, group_rows, chan_dev), lambda t: (0, t, 0, 0)),
            pl.BlockSpec((1, longitudes, chan_dev), lambda t: (t, 0, 0)),
            whole((longitudes, 2 * orders)),
            whole((1, orders)),
            whole(place.shape),
        ],
        out_specs=pl.BlockSpec((1, longitudes, chan_dev), lambda t: (t, 0, 0)),
        out_shape=jax.ShapeDtypeStruct(grid_input.shape, jnp.bfloat16),
        compiler_params=params,
    )(back, grid_input, jnp.asarray(table), order_row, place)


def solution(mesh):
    placed = (
        P(("groups", "lat"), None, "chan"),
        P(("lat", "chan"), None, None),
        P(None, "lat"),
        P(),
        P(),
    )
    return jax.shard_map(
        shards,
        mesh=mesh,
        in_specs=placed,
        out_specs=P(("groups", "lat"), None, "chan"),
        check_vma=False,
    )
```

```python
import functools
import math

import jax
import jax.numpy as jnp
import numpy as np
from jax import lax
from jax.experimental import pallas as pl
from jax.experimental.pallas import tpu as pltpu
from jax.sharding import PartitionSpec as P

MIB = 1024 * 1024


def transform_tables(orders, longitudes):
    residue = np.arange(longitudes)[:, None] * np.arange(orders)[None, :] % longitudes
    angle = residue.astype(np.float32) * np.float32(2.0 * math.pi / longitudes)
    scale = np.float32(1.0 / math.sqrt(longitudes))
    forward = np.concatenate([np.cos(angle) * scale, -np.sin(angle) * scale], axis=1)
    weight = np.where(np.arange(2 * orders) % orders == 0, 1.0, 2.0).astype(np.float32)
    return forward.astype(jnp.bfloat16), (forward * weight).astype(jnp.bfloat16)


def grouped_columns(orders, groups):
    return np.arange(2 * orders).reshape(2, groups, orders // groups).transpose(1, 0, 2).reshape(-1)


def analysis_kernel(
    factor, chunk, grid_hbm, table_hbm, legendre_hbm, gain_hbm, slot_hbm, out_ref,
    grid_buf, table_buf, legendre_buf, gain_buf, slot_buf, grid_sem, table_sem, small_sem,
):
    lat_count, groups, _, _ = out_ref.shape
    lat_dev, longitudes, channels = grid_buf.shape
    slot_count, latitudes, degrees = legendre_buf.shape
    orders = slot_buf.shape[1]
    group_orders = orders // groups
    group_rows = 2 * group_orders
    chunks = longitudes // chunk
    small = [
        pltpu.make_async_copy(src, dst, small_sem.at[i])
        for i, (src, dst) in enumerate(((legendre_hbm, legendre_buf), (gain_hbm, gain_buf), (slot_hbm, slot_buf)))
    ]
    tables = [pltpu.make_async_copy(table_hbm.at[k], table_buf.at[k], table_sem.at[k]) for k in range(chunks)]
    parts = [
        [
            pltpu.make_async_copy(
                grid_hbm.at[t, pl.ds(k * chunk, chunk)], grid_buf.at[t, pl.ds(k * chunk, chunk)], grid_sem.at[t, k]
            )
            for k in range(chunks)
        ]
        for t in range(lat_dev)
    ]
    for copy in small:
        copy.start()
    for k in range(chunks):
        tables[k].start()
        parts[0][k].start()
    for t in range(1, lat_dev):
        for k in range(chunks):
            parts[t][k].start()

    for copy in small:
        copy.wait()
    lanes = 2 * latitudes * latitudes
    own = (lax.axis_index("lat") * lax.axis_size("chan") + lax.axis_index("chan")) * slot_count
    block = lax.broadcasted_iota(jnp.int32, (1, degrees), 1) // 64
    high_lane = lax.broadcasted_iota(jnp.int32, (1, lanes), 1) < lanes // 2
    row = lax.broadcasted_iota(jnp.int32, (group_orders, lanes), 0)
    placed = [jnp.zeros((group_orders, lanes), jnp.float32) for _ in range(groups)]
    for s in range(slot_count):
        order = slot_buf[0, own + s]
        rows = legendre_buf[s].astype(jnp.float32)
        products = [rows * rows[v : v + 1] for v in range(latitudes)] * 2
        weights = jnp.where(block >= order // 64, gain_buf[...] * factor, 0.0)
        pair = lax.dot_general(
            weights,
            jnp.concatenate(products, axis=0),
            (((1,), (1,)), ((), ())),
            precision=lax.Precision.HIGHEST,
            preferred_element_type=jnp.float32,
        )
        high = pair.astype(jnp.bfloat16).astype(jnp.float32)
        pair = jnp.where(high_lane, high, pair - high)
        for g in range(groups):
            placed[g] = jnp.where(row == order - g * group_orders, pair, placed[g])
    top = lat_dev * group_rows * (channels // 128)
    for g in range(groups):
        value = placed[g].astype(jnp.bfloat16)
        for a in range(lat_count):
            out_ref[a, g, top : top + group_orders] = value

    for t in range(lat_dev):
        total = None
        for k in range(chunks):
            if t == 0:
                tables[k].wait()
            parts[t][k].wait()
            term = jnp.dot(
                table_buf[k], grid_buf[t, k * chunk : (k + 1) * chunk, :], preferred_element_type=jnp.float32
            )
            total = term if total is None else total + term
        spectrum = total.astype(jnp.bfloat16)
        for g in range(groups):
            for h in range(channels // 128):
                value = spectrum[g * group_rows : (g + 1) * group_rows, h * 128 : (h + 1) * 128]
                at = (h * lat_dev + t) * group_rows
                for a in range(lat_count):
                    out_ref[a, g, at : at + group_rows] = value


def mixing_helpers(latitudes, group_orders):
    row = np.arange(latitudes * 2 * group_orders)
    t, rm = row // (2 * group_orders), row % (2 * group_orders)
    lane = np.arange(2 * latitudes * latitudes)
    part, lane_v, lane_t = lane // latitudes**2, lane // latitudes % latitudes, lane % latitudes
    keep = t[:, None] == lane_v[None, :]
    spread = lane_t[:, None] == t[None, :]
    halves = np.concatenate([spread & (part == 0)[:, None], spread & (part == 1)[:, None]], axis=1)
    same = rm[:, None] == rm[None, :]
    return [m.astype(jnp.bfloat16) for m in (keep, halves, same)]


def mixing_kernel(lat_dev, rows_ref, weight_ref, keep_ref, halves_ref, same_ref, *out_and_scratch):
    outs, held = out_and_scratch[:-1], out_and_scratch[-1]
    lat_count, chan_count, _, _ = rows_ref.shape
    count = same_ref.shape[0]
    part_rows = count // lat_count
    lanes = keep_ref.shape[1]
    channels = weight_ref.shape[0] // chan_count
    split = channels // 128
    group_orders = rows_ref.shape[2] - split * part_rows
    mixed = None
    pairs = None
    for b in range(chan_count):
        block = jnp.concatenate(
            [rows_ref[:, b, h * part_rows : (h + 1) * part_rows, :].reshape(count, 128) for h in range(split)], axis=1
        )
        term = jnp.dot(
            block, weight_ref[b * channels : (b + 1) * channels, :], preferred_element_type=jnp.float32
        )
        mixed = term if mixed is None else mixed + term
        for a in range(lat_count):
            sent = rows_ref[a, b, split * part_rows :, :].astype(jnp.float32)
            pairs = sent if pairs is None else pairs + sent
    wide = jnp.concatenate([pairs] * (count // group_orders), axis=0) * keep_ref[...].astype(jnp.float32)
    matrix = jnp.dot(wide.astype(jnp.bfloat16), halves_ref[...], preferred_element_type=jnp.float32)
    same = same_ref[...].astype(jnp.float32)
    high = (matrix[:, :count] * same).astype(jnp.bfloat16)
    low = (matrix[:, count:] * same).astype(jnp.bfloat16)
    mixed_high = mixed.astype(jnp.bfloat16)
    mixed_low = (mixed - mixed_high.astype(jnp.float32)).astype(jnp.bfloat16)
    synthesis = (
        jnp.dot(high, mixed_high, preferred_element_type=jnp.float32)
        + jnp.dot(high, mixed_low, preferred_element_type=jnp.float32)
        + jnp.dot(low, mixed_high, preferred_element_type=jnp.float32)
    )
    held[...] = synthesis.astype(jnp.bfloat16).reshape(held.shape)
    for s in range(lat_count):
        outs[s][...] = held[lax.rem(lax.axis_index("chan") + s, lat_count)]


def synthesis_kernel(groups, *refs):
    received = refs[:groups]
    grid_ref, table_ref, out_ref, held = refs[groups:]
    lat_dev = grid_ref.shape[0]
    group_rows = held.shape[2]
    channels = held.shape[3]

    @pl.when(pl.program_id(0) == 0)
    def _():
        for s in range(groups):
            group = lax.rem(lax.axis_index("lat") + groups - s, groups)
            for t in range(lat_dev):
                held[t, group] = received[s][t * group_rows : (t + 1) * group_rows, :]

    for t in range(lat_dev):
        rows = held[t].reshape(groups * group_rows, channels)
        field = jnp.dot(table_ref[...], rows, preferred_element_type=jnp.float32)
        inner = math.sqrt(2.0 / math.pi) * (field + 0.044715 * (field * field * field))
        value = grid_ref[t].astype(jnp.float32) + 0.5 * field * (1.0 + jnp.tanh(inner))
        out_ref[t] = value.astype(jnp.bfloat16)


def chunk_of(longitudes):
    return max(n for n in range(16, 481, 16) if longitudes % n == 0)


def compact_shards(grid_input, legendre, mix_weight, degree_gain, order_slot):
    lat_dev, longitudes, channels = grid_input.shape
    orders = order_slot.shape[0]
    slot_count, degrees, latitudes = legendre.shape
    lat_count = lax.axis_size("lat")
    groups = lax.axis_size("chan")
    group_orders = orders // groups
    group_rows = 2 * group_orders
    part_rows = lat_dev * group_rows
    block_rows = part_rows * (channels // 128) + group_orders
    chunk = chunk_of(longitudes)
    chunks = longitudes // chunk
    columns = grouped_columns(orders, groups)
    forward, inverse = (table[:, columns] for table in transform_tables(orders, longitudes))
    forward = np.ascontiguousarray(forward.reshape(chunks, chunk, 2 * orders).transpose(0, 2, 1))
    hbm = pl.BlockSpec(memory_space=pltpu.HBM)

    sent = pl.pallas_call(
        functools.partial(analysis_kernel, math.sqrt(latitudes / degrees), chunk),
        in_specs=[hbm] * 5,
        out_shape=jax.ShapeDtypeStruct((lat_count, groups, block_rows, 128), jnp.bfloat16),
        scratch_shapes=[
            pltpu.VMEM(grid_input.shape, jnp.bfloat16),
            pltpu.VMEM(forward.shape, jnp.bfloat16),
            pltpu.VMEM((slot_count, latitudes, degrees), jnp.bfloat16),
            pltpu.VMEM((1, degrees), jnp.float32),
            pltpu.SMEM((1, orders), jnp.int32),
            pltpu.SemaphoreType.DMA((lat_dev, chunks)),
            pltpu.SemaphoreType.DMA((chunks,)),
            pltpu.SemaphoreType.DMA((3,)),
        ],
        compiler_params=pltpu.CompilerParams(vmem_limit_bytes=24 * MIB),
    )(
        grid_input,
        jnp.asarray(forward),
        jnp.swapaxes(legendre, 1, 2),
        degree_gain.reshape(1, degrees),
        order_slot.reshape(1, orders),
    )
    rows = lax.all_to_all(
        sent.reshape(lat_count * groups, block_rows, 128), ("lat", "chan"), split_axis=0, concat_axis=0, tiled=True
    )

    helpers = [jnp.asarray(m) for m in mixing_helpers(latitudes, group_orders)]
    columns_here = mix_weight.shape[1]
    parts = pl.pallas_call(
        functools.partial(mixing_kernel, lat_dev),
        out_shape=[jax.ShapeDtypeStruct((part_rows, columns_here), jnp.bfloat16)] * lat_count,
        scratch_shapes=[pltpu.VMEM((lat_count, part_rows, columns_here), jnp.bfloat16)],
        compiler_params=pltpu.CompilerParams(vmem_limit_bytes=24 * MIB),
    )(rows.reshape(lat_count, groups, block_rows, 128), mix_weight, *helpers)

    received = []
    for s in range(lat_count):
        pairs = [
            (a * groups + b, (b + s) % lat_count * groups + a) for a in range(lat_count) for b in range(groups)
        ]
        received.append(lax.ppermute(parts[s], ("lat", "chan"), pairs))

    return pl.pallas_call(
        functools.partial(synthesis_kernel, groups),
        grid=(chunks,),
        in_specs=[pl.BlockSpec((part_rows, channels), lambda k: (0, 0))] * lat_count
        + [
            pl.BlockSpec((lat_dev, chunk, channels), lambda k: (0, k, 0)),
            pl.BlockSpec((chunk, 2 * orders), lambda k: (k, 0)),
        ],
        out_specs=pl.BlockSpec((lat_dev, chunk, channels), lambda k: (0, k, 0)),
        out_shape=jax.ShapeDtypeStruct(grid_input.shape, jnp.bfloat16),
        scratch_shapes=[pltpu.VMEM((lat_dev, groups, group_rows, channels), jnp.bfloat16)],
        compiler_params=pltpu.CompilerParams(vmem_limit_bytes=24 * MIB),
    )(*received, grid_input, jnp.asarray(inverse))


def wide_shards(grid_input, legendre, mix_weight, degree_gain, order_slot):
    lat_dev, longitudes, channels = grid_input.shape
    orders = order_slot.shape[0]
    slot_count, degrees, latitudes = legendre.shape
    lat_count = lax.axis_size("lat")
    chan_count = lax.axis_size("chan")
    group_slots = lat_count * slot_count
    forward, inverse = (jnp.asarray(table) for table in transform_tables(orders, longitudes))

    own = (lax.axis_index("lat") * chan_count + lax.axis_index("chan")) * slot_count
    first_block = lax.dynamic_slice_in_dim(order_slot, own, slot_count, 0) // 64
    alive = jnp.arange(degrees, dtype=jnp.int32)[None, :] // 64 >= first_block[:, None]
    weights = jnp.where(alive, degree_gain[None, :] * math.sqrt(latitudes / degrees), 0.0)
    table = legendre.astype(jnp.float32)
    pairs = jnp.einsum("slv,slt->svt", table * weights[:, :, None], table, precision=lax.Precision.HIGHEST)

    slots = jnp.arange(orders, dtype=jnp.int32).reshape(lat_count, chan_count, slot_count).transpose(1, 0, 2)
    order_of_place = jnp.take(order_slot, slots.reshape(orders))
    hit = order_of_place[:, None] == jnp.arange(orders, dtype=jnp.int32)[None, :]
    hit = hit.astype(jnp.bfloat16)

    spectrum = jnp.einsum("akc,kn->anc", grid_input, forward, preferred_element_type=jnp.float32)
    spectrum = spectrum.astype(jnp.bfloat16).reshape(lat_dev, 2, orders, channels)
    rows = jnp.einsum("pm,armc->parc", hit, spectrum).astype(jnp.bfloat16)
    rows = rows.reshape(chan_count, group_slots, lat_dev, 2, channels)
    rows = lax.all_to_all(rows, "chan", split_axis=0, concat_axis=0, tiled=True)
    rows = lax.all_gather(rows, "lat", axis=0)
    pairs = lax.all_gather(pairs, "lat", axis=0, tiled=True)

    mixed = jnp.einsum(
        "absurc,bcd->sraud",
        rows,
        mix_weight.reshape(chan_count, channels, -1),
        preferred_element_type=jnp.float32,
    )
    mixed = mixed.reshape(group_slots, 2, latitudes, -1)
    synthesis = jnp.einsum("svt,srtd->vsrd", pairs, mixed, precision=lax.Precision.HIGHEST).astype(jnp.bfloat16)

    synthesis = synthesis.reshape(lat_count, lat_dev, group_slots, 2, -1)
    back = lax.all_to_all(synthesis, "lat", split_axis=0, concat_axis=0, tiled=True)
    back = back.transpose(1, 2, 3, 0, 4).reshape(lat_dev, group_slots, 2, chan_count, channels)
    back = lax.all_to_all(back.transpose(3, 0, 1, 2, 4), "chan", split_axis=0, concat_axis=0, tiled=True)
    back = back.transpose(1, 0, 2, 3, 4).reshape(lat_dev, orders, 2, channels)
    natural = jnp.einsum("pm,aprc->armc", hit, back).astype(jnp.bfloat16)
    field = jnp.einsum(
        "anc,kn->akc",
        natural.reshape(lat_dev, 2 * orders, channels),
        inverse,
        preferred_element_type=jnp.float32,
    )
    return (grid_input.astype(jnp.float32) + jax.nn.gelu(field)).astype(jnp.bfloat16)


def shards(grid_input, legendre, mix_weight, degree_gain, order_slot):
    lat_count, chan_count = lax.axis_size("lat"), lax.axis_size("chan")
    orders, latitudes = order_slot.shape[0], legendre.shape[2]
    compact = (
        lat_count == chan_count
        and 2 * latitudes * latitudes == 128
        and orders % (16 * chan_count) == 0
        and grid_input.shape[2] % 128 == 0
        and grid_input.shape[1] % 16 == 0
    )
    body = compact_shards if compact else wide_shards
    return body(grid_input, legendre, mix_weight, degree_gain, order_slot)


def solution(mesh):
    placed = (
        P(("groups", "lat"), None, "chan"),
        P(("lat", "chan"), None, None),
        P(None, "lat"),
        P(),
        P(),
    )
    return jax.shard_map(
        shards,
        mesh=mesh,
        in_specs=placed,
        out_specs=P(("groups", "lat"), None, "chan"),
        check_vma=False,
    )
```

```python
import functools
import math

import jax
import jax.numpy as jnp
import numpy as np
from jax import lax
from jax.experimental import pallas as pl
from jax.experimental.pallas import tpu as pltpu
from jax.sharding import PartitionSpec as P

MIB = 1024 * 1024
ROOT = math.sqrt(2.0 / math.pi)


def transform_tables(orders, longitudes):
    residue = np.arange(longitudes)[:, None] * np.arange(orders)[None, :] % longitudes
    angle = residue.astype(np.float32) * np.float32(2.0 * math.pi / longitudes)
    scale = np.float32(1.0 / math.sqrt(longitudes))
    forward = np.concatenate([np.cos(angle) * scale, -np.sin(angle) * scale], axis=1)
    weight = np.where(np.arange(2 * orders) % orders == 0, 0.5, 1.0).astype(np.float32)
    return forward.astype(jnp.bfloat16), (forward * weight).astype(jnp.bfloat16)


def grouped_columns(orders, groups):
    return np.arange(2 * orders).reshape(2, groups, orders // groups).transpose(1, 0, 2).reshape(-1)


def analysis_kernel(
    factor, chunk, grid_hbm, table_hbm, legendre_hbm, gain_hbm, slot_hbm, out_ref,
    grid_buf, table_buf, legendre_buf, gain_buf, slot_buf, grid_sem, table_sem, small_sem,
):
    lat_count, chips, _, _ = out_ref.shape
    groups = 2 * chips
    lat_dev, longitudes, channels = grid_buf.shape
    slot_count, latitudes, degrees = legendre_buf.shape
    orders = slot_buf.shape[1]
    group_orders = orders // groups
    group_rows = 2 * group_orders
    chunks = longitudes // chunk
    small = [
        pltpu.make_async_copy(src, dst, small_sem.at[i])
        for i, (src, dst) in enumerate(((legendre_hbm, legendre_buf), (gain_hbm, gain_buf), (slot_hbm, slot_buf)))
    ]
    tables = [pltpu.make_async_copy(table_hbm.at[k], table_buf.at[k], table_sem.at[k]) for k in range(chunks)]
    parts = [
        [
            pltpu.make_async_copy(
                grid_hbm.at[t, pl.ds(k * chunk, chunk)], grid_buf.at[t, pl.ds(k * chunk, chunk)], grid_sem.at[t, k]
            )
            for k in range(chunks)
        ]
        for t in range(lat_dev)
    ]
    for copy in small:
        copy.start()
    for k in range(chunks):
        tables[k].start()
        parts[0][k].start()
    for t in range(1, lat_dev):
        for k in range(chunks):
            parts[t][k].start()

    for copy in small:
        copy.wait()
    lanes = 2 * latitudes * latitudes
    own = (lax.axis_index("lat") * lax.axis_size("chan") + lax.axis_index("chan")) * slot_count
    block = lax.broadcasted_iota(jnp.int32, (1, degrees), 1) // 64
    high_lane = lax.broadcasted_iota(jnp.int32, (1, lanes), 1) < lanes // 2
    row = lax.broadcasted_iota(jnp.int32, (group_orders, lanes), 0)
    sums = []
    for s in range(slot_count):
        rows = legendre_buf[s].astype(jnp.float32)
        weights = jnp.where(block >= slot_buf[0, own + s] // 64, gain_buf[...] * factor, 0.0)
        weighted = rows * weights
        terms = jnp.concatenate([weighted * rows[v : v + 1] for v in range(latitudes)], axis=0)
        sums += [sum(terms[:, k : k + 128] for k in range(0, degrees, 128))] * 2
    sums = jnp.concatenate(sums, axis=0)
    high = sums.astype(jnp.bfloat16)
    low = (sums - high.astype(jnp.float32)).astype(jnp.bfloat16)
    pairs = lax.dot_general(
        jnp.ones((8, 256), jnp.bfloat16),
        jnp.concatenate([high, low], axis=1),
        (((1,), (1,)), ((), ())),
        preferred_element_type=jnp.float32,
    )
    placed = [jnp.zeros((group_orders, lanes), jnp.float32) for _ in range(groups)]
    for s in range(slot_count):
        order = slot_buf[0, own + s]
        pair = pairs[:1, s * lanes : (s + 1) * lanes]
        high = pair.astype(jnp.bfloat16).astype(jnp.float32)
        pair = jnp.where(high_lane, high, pair - high)
        for g in range(groups):
            placed[g] = jnp.where(row == order - g * group_orders, pair, placed[g])
    top = lat_dev * group_rows * (channels // 128)
    for g in range(groups):
        value = placed[g].astype(jnp.bfloat16)
        for a in range(g // chips, lat_count, 2):
            out_ref[a, g % chips, top : top + group_orders] = value

    for t in range(lat_dev):
        total = None
        for k in range(chunks):
            if t == 0:
                tables[k].wait()
            parts[t][k].wait()
            term = jnp.dot(
                table_buf[k], grid_buf[t, k * chunk : (k + 1) * chunk, :], preferred_element_type=jnp.float32
            )
            total = term if total is None else total + term
        spectrum = total.astype(jnp.bfloat16)
        for g in range(groups):
            for h in range(channels // 128):
                value = spectrum[g * group_rows : (g + 1) * group_rows, h * 128 : (h + 1) * 128]
                at = (h * lat_dev + t) * group_rows
                for a in range(g // chips, lat_count, 2):
                    out_ref[a, g % chips, at : at + group_rows] = value


def mixing_helpers(latitudes, group_orders):
    row = np.arange(latitudes * 2 * group_orders)
    t, rm = row // (2 * group_orders), row % (2 * group_orders)
    lane = np.arange(2 * latitudes * latitudes)
    part, lane_v, lane_t = lane // latitudes**2, lane // latitudes % latitudes, lane % latitudes
    keep = t[:, None] == lane_v[None, :]
    spread = lane_t[:, None] == t[None, :]
    halves = np.concatenate([spread & (part == 0)[:, None], spread & (part == 1)[:, None]], axis=1)
    same = rm[:, None] == rm[None, :]
    return [m.astype(jnp.bfloat16) for m in (keep, halves, same)]


def choose_kernel(weight_ref, moved_ref, out_ref):
    own = lax.rem(lax.axis_index("lat") + lax.axis_index("chan"), 2) == 0

    @pl.when(own)
    def _():
        out_ref[...] = weight_ref[...]

    @pl.when(jnp.logical_not(own))
    def _():
        out_ref[...] = moved_ref[...]


def mixing_kernel(own_ref, other_ref, weight_ref, keep_ref, halves_ref, same_ref, out_ref):
    lat_count, chips, block_rows, _ = own_ref.shape
    count = same_ref.shape[0]
    part_rows = count // lat_count
    channels = weight_ref.shape[0] // (2 * chips)
    split = channels // 128
    group_orders = block_rows - split * part_rows
    core = lax.rem(lax.axis_index("chan"), 2)
    mixed = None
    pairs = None
    for x in range(chips):
        for rows_ref, sender in ((own_ref, core), (other_ref, 1 - core)):
            block = jnp.concatenate(
                [rows_ref[:, x, h * part_rows : (h + 1) * part_rows, :].reshape(count, 128) for h in range(split)],
                axis=1,
            )
            at = pl.ds(pl.multiple_of((2 * x + sender) * channels, channels), channels)
            term = jnp.dot(block, weight_ref[at, :], preferred_element_type=jnp.float32)
            mixed = term if mixed is None else mixed + term
            for a in range(lat_count):
                sent = rows_ref[a, x, split * part_rows :, :].astype(jnp.float32)
                pairs = sent if pairs is None else pairs + sent
    wide = jnp.concatenate([pairs] * (count // group_orders), axis=0) * keep_ref[...].astype(jnp.float32)
    matrix = jnp.dot(wide.astype(jnp.bfloat16), halves_ref[...], preferred_element_type=jnp.float32)
    same = same_ref[...].astype(jnp.float32)
    high = (matrix[:, :count] * same).astype(jnp.bfloat16)
    low = (matrix[:, count:] * same).astype(jnp.bfloat16)
    mixed_high = mixed.astype(jnp.bfloat16)
    mixed_low = (mixed - mixed_high.astype(jnp.float32)).astype(jnp.bfloat16)
    synthesis = (
        jnp.dot(high, mixed_high, preferred_element_type=jnp.float32)
        + jnp.dot(high, mixed_low, preferred_element_type=jnp.float32)
        + jnp.dot(low, mixed_high, preferred_element_type=jnp.float32)
    )
    out_ref[...] = jnp.zeros(out_ref.shape, out_ref.dtype)
    to_chip = lax.axis_index("lat") // 2
    out_ref[:, to_chip] = synthesis.astype(jnp.bfloat16).reshape((lat_count,) + out_ref.shape[2:])


def synthesis_kernel(piece, received_ref, grid_ref, table_ref, out_hbm, out_buf, out_sem):
    lat_dev, longitudes, channels = grid_ref.shape
    _, chips, part_rows, _ = received_ref.shape
    group_rows = part_rows // lat_dev
    pair = lax.axis_index("chan") // 2 * 2
    parts = out_sem.shape[1]
    size = longitudes // parts
    copies = []
    for t in range(lat_dev):
        rows = jnp.concatenate(
            [
                received_ref[pair + g, x, t * group_rows : (t + 1) * group_rows, :]
                for g in range(2)
                for x in range(chips)
            ],
            axis=0,
        )
        for k in range(parts):
            for at in range(k * size, (k + 1) * size, piece):
                half = jnp.dot(table_ref[at : at + piece, :], rows, preferred_element_type=jnp.float32)
                square = half * half
                inner = half * (2.0 * ROOT + (8.0 * ROOT * 0.044715) * square)
                value = grid_ref[t, at : at + piece, :].astype(jnp.float32) + half * (1.0 + jnp.tanh(inner))
                out_buf[t, at : at + piece, :] = value.astype(jnp.bfloat16)
            span = pl.ds(k * size, size)
            copy = pltpu.make_async_copy(out_buf.at[t, span], out_hbm.at[t, span], out_sem.at[t, k])
            copy.start()
            copies.append(copy)
    for copy in copies:
        copy.wait()


def chunk_of(longitudes):
    return max(n for n in range(16, 481, 16) if longitudes % n == 0)


def compact_shards(grid_input, legendre, mix_weight, degree_gain, order_slot):
    lat_dev, longitudes, channels = grid_input.shape
    orders = order_slot.shape[0]
    slot_count, degrees, latitudes = legendre.shape
    lat_count = lax.axis_size("lat")
    groups = lax.axis_size("chan")
    chips = groups // 2
    group_orders = orders // groups
    group_rows = 2 * group_orders
    part_rows = lat_dev * group_rows
    block_rows = part_rows * (channels // 128) + group_orders
    chunk = chunk_of(longitudes)
    chunks = longitudes // chunk
    columns = grouped_columns(orders, groups)
    forward, inverse = (table[:, columns] for table in transform_tables(orders, longitudes))
    forward = np.ascontiguousarray(forward.reshape(chunks, chunk, 2 * orders).transpose(0, 2, 1))
    hbm = pl.BlockSpec(memory_space=pltpu.HBM)

    both = ("lat", "chan")
    places = [(a, b) for a in range(lat_count) for b in range(groups)]
    moved = lax.ppermute(
        mix_weight, both, [(a * groups + b, (a ^ 1) * groups + b) for a, b in places if (a + b) % 2 == 0]
    )

    weight = pl.pallas_call(
        choose_kernel,
        out_shape=jax.ShapeDtypeStruct(mix_weight.shape, jnp.bfloat16),
        cost_estimate=pl.CostEstimate(flops=100000000000, bytes_accessed=100000000, transcendentals=0),
        compiler_params=pltpu.CompilerParams(vmem_limit_bytes=24 * MIB),
    )(mix_weight, moved)

    sent = pl.pallas_call(
        functools.partial(analysis_kernel, math.sqrt(latitudes / degrees), chunk),
        in_specs=[hbm] * 5,
        out_shape=pltpu.VMEM((lat_count, chips, block_rows, 128), jnp.bfloat16),
        scratch_shapes=[
            pltpu.VMEM(grid_input.shape, jnp.bfloat16),
            pltpu.VMEM(forward.shape, jnp.bfloat16),
            pltpu.VMEM((slot_count, latitudes, degrees), jnp.bfloat16),
            pltpu.VMEM((1, degrees), jnp.float32),
            pltpu.SMEM((1, orders), jnp.int32),
            pltpu.SemaphoreType.DMA((lat_dev, chunks)),
            pltpu.SemaphoreType.DMA((chunks,)),
            pltpu.SemaphoreType.DMA((3,)),
        ],
        compiler_params=pltpu.CompilerParams(vmem_limit_bytes=24 * MIB),
    )(
        *(
            pltpu.with_memory_space_constraint(operand, pltpu.HBM)
            for operand in (
                grid_input,
                jnp.asarray(forward),
                jnp.swapaxes(legendre, 1, 2),
                degree_gain.reshape(1, degrees),
                order_slot.reshape(1, orders),
            )
        )
    )
    cores = [[a * groups + 2 * x + k for a in range(lat_count) for x in range(chips)] for k in range(2)]
    own = lax.all_to_all(
        sent.reshape(lat_count * chips, block_rows, 128),
        both,
        split_axis=0,
        concat_axis=0,
        tiled=True,
        axis_index_groups=cores,
    )
    other = lax.ppermute(own, both, [(n, n ^ 1) for n in range(lat_count * groups)])

    helpers = [jnp.asarray(m) for m in mixing_helpers(latitudes, group_orders)]
    columns_here = mix_weight.shape[1]
    parts = pl.pallas_call(
        mixing_kernel,
        out_shape=jax.ShapeDtypeStruct((lat_count, chips, part_rows, columns_here), jnp.bfloat16),
        compiler_params=pltpu.CompilerParams(vmem_limit_bytes=24 * MIB),
    )(*(rows.reshape(lat_count, chips, block_rows, 128) for rows in (own, other)), weight, *helpers)
    received = lax.all_to_all(
        parts.reshape(lat_count * chips, part_rows, columns_here),
        both,
        split_axis=0,
        concat_axis=0,
        tiled=True,
        axis_index_groups=cores,
    ).reshape(lat_count, chips, part_rows, columns_here)

    whole = pl.BlockSpec(memory_space=pltpu.VMEM)
    return pl.pallas_call(
        functools.partial(synthesis_kernel, 96),
        in_specs=[whole] * 3,
        out_specs=hbm,
        out_shape=jax.ShapeDtypeStruct(grid_input.shape, jnp.bfloat16),
        scratch_shapes=[
            pltpu.VMEM(grid_input.shape, jnp.bfloat16),
            pltpu.SemaphoreType.DMA((lat_dev, 3)),
        ],
        compiler_params=pltpu.CompilerParams(vmem_limit_bytes=24 * MIB),
    )(received, grid_input, jnp.asarray(inverse))


def wide_shards(grid_input, legendre, mix_weight, degree_gain, order_slot):
    lat_dev, longitudes, channels = grid_input.shape
    orders = order_slot.shape[0]
    slot_count, degrees, latitudes = legendre.shape
    lat_count = lax.axis_size("lat")
    chan_count = lax.axis_size("chan")
    group_slots = lat_count * slot_count
    forward, inverse = (jnp.asarray(table) for table in transform_tables(orders, longitudes))

    own = (lax.axis_index("lat") * chan_count + lax.axis_index("chan")) * slot_count
    first_block = lax.dynamic_slice_in_dim(order_slot, own, slot_count, 0) // 64
    alive = jnp.arange(degrees, dtype=jnp.int32)[None, :] // 64 >= first_block[:, None]
    weights = jnp.where(alive, degree_gain[None, :] * math.sqrt(latitudes / degrees), 0.0)
    table = legendre.astype(jnp.float32)
    pairs = jnp.einsum("slv,slt->svt", table * weights[:, :, None], table, precision=lax.Precision.HIGHEST)

    slots = jnp.arange(orders, dtype=jnp.int32).reshape(lat_count, chan_count, slot_count).transpose(1, 0, 2)
    order_of_place = jnp.take(order_slot, slots.reshape(orders))
    hit = order_of_place[:, None] == jnp.arange(orders, dtype=jnp.int32)[None, :]
    hit = hit.astype(jnp.bfloat16)

    spectrum = jnp.einsum("akc,kn->anc", grid_input, forward, preferred_element_type=jnp.float32)
    spectrum = spectrum.astype(jnp.bfloat16).reshape(lat_dev, 2, orders, channels)
    rows = jnp.einsum("pm,armc->parc", hit, spectrum).astype(jnp.bfloat16)
    rows = rows.reshape(chan_count, group_slots, lat_dev, 2, channels)
    rows = lax.all_to_all(rows, "chan", split_axis=0, concat_axis=0, tiled=True)
    rows = lax.all_gather(rows, "lat", axis=0)
    pairs = lax.all_gather(pairs, "lat", axis=0, tiled=True)

    mixed = jnp.einsum(
        "absurc,bcd->sraud",
        rows,
        mix_weight.reshape(chan_count, channels, -1),
        preferred_element_type=jnp.float32,
    )
    mixed = mixed.reshape(group_slots, 2, latitudes, -1)
    synthesis = jnp.einsum("svt,srtd->vsrd", pairs, mixed, precision=lax.Precision.HIGHEST).astype(jnp.bfloat16)

    synthesis = synthesis.reshape(lat_count, lat_dev, group_slots, 2, -1)
    back = lax.all_to_all(synthesis, "lat", split_axis=0, concat_axis=0, tiled=True)
    back = back.transpose(1, 2, 3, 0, 4).reshape(lat_dev, group_slots, 2, chan_count, channels)
    back = lax.all_to_all(back.transpose(3, 0, 1, 2, 4), "chan", split_axis=0, concat_axis=0, tiled=True)
    back = back.transpose(1, 0, 2, 3, 4).reshape(lat_dev, orders, 2, channels)
    natural = jnp.einsum("pm,aprc->armc", hit, back).astype(jnp.bfloat16)
    field = 2.0 * jnp.einsum(
        "anc,kn->akc",
        natural.reshape(lat_dev, 2 * orders, channels),
        inverse,
        preferred_element_type=jnp.float32,
    )
    return (grid_input.astype(jnp.float32) + jax.nn.gelu(field)).astype(jnp.bfloat16)


def shards(grid_input, legendre, mix_weight, degree_gain, order_slot):
    lat_count, chan_count = lax.axis_size("lat"), lax.axis_size("chan")
    orders, latitudes = order_slot.shape[0], legendre.shape[2]
    compact = (
        lat_count == chan_count
        and chan_count % 2 == 0
        and 2 * latitudes * latitudes == 128
        and orders % (16 * chan_count) == 0
        and grid_input.shape[2] % 128 == 0
        and grid_input.shape[1] % 16 == 0
    )
    body = compact_shards if compact else wide_shards
    return body(grid_input, legendre, mix_weight, degree_gain, order_slot)


def solution(mesh):
    placed = (
        P(("groups", "lat"), None, "chan"),
        P(("lat", "chan"), None, None),
        P(None, "lat"),
        P(),
        P(),
    )
    return jax.shard_map(
        shards,
        mesh=mesh,
        in_specs=placed,
        out_specs=P(("groups", "lat"), None, "chan"),
        check_vma=False,
    )
```

```python
import functools
import math

import jax
import jax.numpy as jnp
import numpy as np
from jax import lax
from jax.experimental import pallas as pl
from jax.experimental.pallas import tpu as pltpu
from jax.sharding import PartitionSpec as P

MIB = 1024 * 1024
STEPS = (3, 1, 2, 0)
ROOT = math.sqrt(2.0 / math.pi)


def transform_tables(orders, longitudes):
    residue = np.arange(longitudes)[:, None] * np.arange(orders)[None, :] % longitudes
    angle = residue.astype(np.float32) * np.float32(2.0 * math.pi / longitudes)
    scale = np.float32(1.0 / math.sqrt(longitudes))
    forward = np.concatenate([np.cos(angle) * scale, -np.sin(angle) * scale], axis=1)
    weight = np.where(np.arange(2 * orders) % orders == 0, 0.5, 1.0).astype(np.float32)
    return forward.astype(jnp.bfloat16), (forward * weight).astype(jnp.bfloat16)


def grouped_columns(orders, groups):
    return np.arange(2 * orders).reshape(2, groups, orders // groups).transpose(1, 0, 2).reshape(-1)


def analysis_kernel(
    factor, chunk, grid_hbm, table_hbm, legendre_hbm, gain_hbm, slot_hbm, out_ref,
    grid_buf, table_buf, legendre_buf, gain_buf, slot_buf, grid_sem, table_sem, small_sem,
):
    lat_count, chips, _, _ = out_ref.shape
    groups = 2 * chips
    lat_dev, longitudes, channels = grid_buf.shape
    slot_count, latitudes, degrees = legendre_buf.shape
    orders = slot_buf.shape[1]
    group_orders = orders // groups
    group_rows = 2 * group_orders
    chunks = longitudes // chunk
    small = [
        pltpu.make_async_copy(src, dst, small_sem.at[i])
        for i, (src, dst) in enumerate(((legendre_hbm, legendre_buf), (gain_hbm, gain_buf), (slot_hbm, slot_buf)))
    ]
    tables = [pltpu.make_async_copy(table_hbm.at[k], table_buf.at[k], table_sem.at[k]) for k in range(chunks)]
    parts = [
        [
            pltpu.make_async_copy(
                grid_hbm.at[t, pl.ds(k * chunk, chunk)], grid_buf.at[t, pl.ds(k * chunk, chunk)], grid_sem.at[t, k]
            )
            for k in range(chunks)
        ]
        for t in range(lat_dev)
    ]
    for copy in small:
        copy.start()
    for k in range(chunks):
        tables[k].start()
        parts[0][k].start()
    for t in range(1, lat_dev):
        for k in range(chunks):
            parts[t][k].start()

    for copy in small:
        copy.wait()
    lanes = 2 * latitudes * latitudes
    own = (lax.axis_index("lat") * lax.axis_size("chan") + lax.axis_index("chan")) * slot_count
    block = lax.broadcasted_iota(jnp.int32, (1, degrees), 1) // 64
    high_lane = lax.broadcasted_iota(jnp.int32, (1, lanes), 1) < lanes // 2
    row = lax.broadcasted_iota(jnp.int32, (group_orders, lanes), 0)
    sums = []
    for s in range(slot_count):
        rows = legendre_buf[s].astype(jnp.float32)
        weights = jnp.where(block >= slot_buf[0, own + s] // 64, gain_buf[...] * factor, 0.0)
        weighted = rows * weights
        terms = jnp.concatenate([weighted * rows[v : v + 1] for v in range(latitudes)], axis=0)
        sums += [sum(terms[:, k : k + 128] for k in range(0, degrees, 128))] * 2
    sums = jnp.concatenate(sums, axis=0)
    high = sums.astype(jnp.bfloat16)
    low = (sums - high.astype(jnp.float32)).astype(jnp.bfloat16)
    pairs = lax.dot_general(
        jnp.ones((8, 256), jnp.bfloat16),
        jnp.concatenate([high, low], axis=1),
        (((1,), (1,)), ((), ())),
        preferred_element_type=jnp.float32,
    )
    placed = [jnp.zeros((group_orders, lanes), jnp.float32) for _ in range(groups)]
    for s in range(slot_count):
        order = slot_buf[0, own + s]
        pair = pairs[:1, s * lanes : (s + 1) * lanes]
        high = pair.astype(jnp.bfloat16).astype(jnp.float32)
        pair = jnp.where(high_lane, high, pair - high)
        for g in range(groups):
            placed[g] = jnp.where(row == order - g * group_orders, pair, placed[g])
    top = lat_dev * group_rows * (channels // 128)
    for g in range(groups):
        value = placed[g].astype(jnp.bfloat16)
        for a in range(g // chips, lat_count, 2):
            out_ref[a, g % chips, top : top + group_orders] = value

    for t in range(lat_dev):
        total = None
        for k in range(chunks):
            if t == 0:
                tables[k].wait()
            parts[t][k].wait()
            term = jnp.dot(
                table_buf[k], grid_buf[t, k * chunk : (k + 1) * chunk, :], preferred_element_type=jnp.float32
            )
            total = term if total is None else total + term
        spectrum = total.astype(jnp.bfloat16)
        for g in range(groups):
            for h in range(channels // 128):
                value = spectrum[g * group_rows : (g + 1) * group_rows, h * 128 : (h + 1) * 128]
                at = (h * lat_dev + t) * group_rows
                for a in range(g // chips, lat_count, 2):
                    out_ref[a, g % chips, at : at + group_rows] = value


def mixing_helpers(latitudes, group_orders):
    row = np.arange(latitudes * 2 * group_orders)
    t, rm = row // (2 * group_orders), row % (2 * group_orders)
    lane = np.arange(2 * latitudes * latitudes)
    part, lane_v, lane_t = lane // latitudes**2, lane // latitudes % latitudes, lane % latitudes
    keep = t[:, None] == lane_v[None, :]
    spread = lane_t[:, None] == t[None, :]
    halves = np.concatenate([spread & (part == 0)[:, None], spread & (part == 1)[:, None]], axis=1)
    same = rm[:, None] == rm[None, :]
    return [m.astype(jnp.bfloat16) for m in (keep, halves, same)]


def choose_kernel(weight_ref, moved_ref, out_ref):
    own = lax.rem(lax.axis_index("lat") + lax.axis_index("chan"), 2) == 0

    @pl.when(own)
    def _():
        out_ref[...] = weight_ref[...]

    @pl.when(jnp.logical_not(own))
    def _():
        out_ref[...] = moved_ref[...]


def mixing_kernel(own_ref, other_ref, weight_ref, keep_ref, halves_ref, same_ref, *out_and_scratch):
    outs, held = out_and_scratch[:-1], out_and_scratch[-1]
    lat_count, chips, block_rows, _ = own_ref.shape
    count = same_ref.shape[0]
    part_rows = count // lat_count
    channels = weight_ref.shape[0] // (2 * chips)
    split = channels // 128
    group_orders = block_rows - split * part_rows
    core = lax.rem(lax.axis_index("chan"), 2)
    mixed = None
    pairs = None
    for x in range(chips):
        for rows_ref, sender in ((own_ref, core), (other_ref, 1 - core)):
            block = jnp.concatenate(
                [rows_ref[:, x, h * part_rows : (h + 1) * part_rows, :].reshape(count, 128) for h in range(split)],
                axis=1,
            )
            at = pl.ds(pl.multiple_of((2 * x + sender) * channels, channels), channels)
            term = jnp.dot(block, weight_ref[at, :], preferred_element_type=jnp.float32)
            mixed = term if mixed is None else mixed + term
            for a in range(lat_count):
                sent = rows_ref[a, x, split * part_rows :, :].astype(jnp.float32)
                pairs = sent if pairs is None else pairs + sent
    wide = jnp.concatenate([pairs] * (count // group_orders), axis=0) * keep_ref[...].astype(jnp.float32)
    matrix = jnp.dot(wide.astype(jnp.bfloat16), halves_ref[...], preferred_element_type=jnp.float32)
    same = same_ref[...].astype(jnp.float32)
    high = (matrix[:, :count] * same).astype(jnp.bfloat16)
    low = (matrix[:, count:] * same).astype(jnp.bfloat16)
    mixed_high = mixed.astype(jnp.bfloat16)
    mixed_low = (mixed - mixed_high.astype(jnp.float32)).astype(jnp.bfloat16)
    synthesis = (
        jnp.dot(high, mixed_high, preferred_element_type=jnp.float32)
        + jnp.dot(high, mixed_low, preferred_element_type=jnp.float32)
        + jnp.dot(low, mixed_high, preferred_element_type=jnp.float32)
    )
    held[...] = synthesis.astype(jnp.bfloat16).reshape(held.shape)
    place = lax.axis_index("chan") - core + lax.rem(lax.axis_index("lat"), 2)
    for step, out_ref in zip(STEPS, outs):
        out_ref[...] = held[place ^ step]


def synthesis_kernel(piece, *refs):
    received = refs[:-6]
    grid_ref, table_ref, out_hbm, held, out_buf, out_sem = refs[-6:]
    lat_dev, longitudes, channels = grid_ref.shape
    groups, part_rows, _ = held.shape
    group_rows = part_rows // lat_dev
    for step, received_ref in zip(STEPS, received):
        sender = lax.axis_index("lat") ^ step
        held[lax.rem(sender, 2) * (groups // 2) + sender // 2] = received_ref[...]
    parts = out_sem.shape[1]
    size = longitudes // parts
    copies = []
    for t in range(lat_dev):
        rows = held[:, t * group_rows : (t + 1) * group_rows, :].reshape(groups * group_rows, channels)
        for k in range(parts):
            for at in range(k * size, (k + 1) * size, piece):
                half = jnp.dot(table_ref[at : at + piece, :], rows, preferred_element_type=jnp.float32)
                square = half * half
                inner = half * (2.0 * ROOT + (8.0 * ROOT * 0.044715) * square)
                value = grid_ref[t, at : at + piece, :].astype(jnp.float32) + half * (1.0 + jnp.tanh(inner))
                out_buf[t, at : at + piece, :] = value.astype(jnp.bfloat16)
            span = pl.ds(k * size, size)
            copy = pltpu.make_async_copy(out_buf.at[t, span], out_hbm.at[t, span], out_sem.at[t, k])
            copy.start()
            copies.append(copy)
    for copy in copies:
        copy.wait()


def chunk_of(longitudes):
    return max(n for n in range(16, 481, 16) if longitudes % n == 0)


def compact_shards(grid_input, legendre, mix_weight, degree_gain, order_slot):
    lat_dev, longitudes, channels = grid_input.shape
    orders = order_slot.shape[0]
    slot_count, degrees, latitudes = legendre.shape
    lat_count = lax.axis_size("lat")
    groups = lax.axis_size("chan")
    chips = groups // 2
    group_orders = orders // groups
    group_rows = 2 * group_orders
    part_rows = lat_dev * group_rows
    block_rows = part_rows * (channels // 128) + group_orders
    chunk = chunk_of(longitudes)
    chunks = longitudes // chunk
    columns = grouped_columns(orders, groups)
    forward, inverse = (table[:, columns] for table in transform_tables(orders, longitudes))
    forward = np.ascontiguousarray(forward.reshape(chunks, chunk, 2 * orders).transpose(0, 2, 1))
    hbm = pl.BlockSpec(memory_space=pltpu.HBM)

    both = ("lat", "chan")
    places = [(a, b) for a in range(lat_count) for b in range(groups)]
    moved = lax.ppermute(
        mix_weight, both, [(a * groups + b, (a ^ 1) * groups + b) for a, b in places if (a + b) % 2 == 0]
    )

    weight = pl.pallas_call(
        choose_kernel,
        out_shape=jax.ShapeDtypeStruct(mix_weight.shape, jnp.bfloat16),
        cost_estimate=pl.CostEstimate(flops=100000000000, bytes_accessed=100000000, transcendentals=0),
        compiler_params=pltpu.CompilerParams(vmem_limit_bytes=24 * MIB),
    )(mix_weight, moved)

    sent = pl.pallas_call(
        functools.partial(analysis_kernel, math.sqrt(latitudes / degrees), chunk),
        in_specs=[hbm] * 5,
        out_shape=pltpu.VMEM((lat_count, chips, block_rows, 128), jnp.bfloat16),
        scratch_shapes=[
            pltpu.VMEM(grid_input.shape, jnp.bfloat16),
            pltpu.VMEM(forward.shape, jnp.bfloat16),
            pltpu.VMEM((slot_count, latitudes, degrees), jnp.bfloat16),
            pltpu.VMEM((1, degrees), jnp.float32),
            pltpu.SMEM((1, orders), jnp.int32),
            pltpu.SemaphoreType.DMA((lat_dev, chunks)),
            pltpu.SemaphoreType.DMA((chunks,)),
            pltpu.SemaphoreType.DMA((3,)),
        ],
        compiler_params=pltpu.CompilerParams(vmem_limit_bytes=24 * MIB),
    )(
        *(
            pltpu.with_memory_space_constraint(operand, pltpu.HBM)
            for operand in (
                grid_input,
                jnp.asarray(forward),
                jnp.swapaxes(legendre, 1, 2),
                degree_gain.reshape(1, degrees),
                order_slot.reshape(1, orders),
            )
        )
    )
    cores = [[a * groups + 2 * x + k for a in range(lat_count) for x in range(chips)] for k in range(2)]
    own = lax.all_to_all(
        sent.reshape(lat_count * chips, block_rows, 128),
        both,
        split_axis=0,
        concat_axis=0,
        tiled=True,
        axis_index_groups=cores,
    )
    other = lax.ppermute(own, both, [(n, n ^ 1) for n in range(lat_count * groups)])

    helpers = [jnp.asarray(m) for m in mixing_helpers(latitudes, group_orders)]
    columns_here = mix_weight.shape[1]
    parts = pl.pallas_call(
        mixing_kernel,
        out_shape=[jax.ShapeDtypeStruct((part_rows, columns_here), jnp.bfloat16)] * lat_count,
        scratch_shapes=[pltpu.VMEM((lat_count, part_rows, columns_here), jnp.bfloat16)],
        compiler_params=pltpu.CompilerParams(vmem_limit_bytes=24 * MIB),
    )(*(rows.reshape(lat_count, chips, block_rows, 128) for rows in (own, other)), weight, *helpers)
    received = []
    for step, part in zip(STEPS, parts):
        pairs = [
            (a * groups + b, ((b // 2 * 2 + a % 2) ^ step) * groups + a // 2 * 2 + b % 2) for a, b in places
        ]
        received.append(lax.ppermute(part, both, pairs))

    whole = pl.BlockSpec(memory_space=pltpu.VMEM)
    return pl.pallas_call(
        functools.partial(synthesis_kernel, 96),
        in_specs=[whole] * (lat_count + 2),
        out_specs=hbm,
        out_shape=jax.ShapeDtypeStruct(grid_input.shape, jnp.bfloat16),
        scratch_shapes=[
            pltpu.VMEM((groups, part_rows, channels), jnp.bfloat16),
            pltpu.VMEM(grid_input.shape, jnp.bfloat16),
            pltpu.SemaphoreType.DMA((lat_dev, 3)),
        ],
        compiler_params=pltpu.CompilerParams(vmem_limit_bytes=24 * MIB),
    )(*received, grid_input, jnp.asarray(inverse))


def wide_shards(grid_input, legendre, mix_weight, degree_gain, order_slot):
    lat_dev, longitudes, channels = grid_input.shape
    orders = order_slot.shape[0]
    slot_count, degrees, latitudes = legendre.shape
    lat_count = lax.axis_size("lat")
    chan_count = lax.axis_size("chan")
    group_slots = lat_count * slot_count
    forward, inverse = (jnp.asarray(table) for table in transform_tables(orders, longitudes))

    own = (lax.axis_index("lat") * chan_count + lax.axis_index("chan")) * slot_count
    first_block = lax.dynamic_slice_in_dim(order_slot, own, slot_count, 0) // 64
    alive = jnp.arange(degrees, dtype=jnp.int32)[None, :] // 64 >= first_block[:, None]
    weights = jnp.where(alive, degree_gain[None, :] * math.sqrt(latitudes / degrees), 0.0)
    table = legendre.astype(jnp.float32)
    pairs = jnp.einsum("slv,slt->svt", table * weights[:, :, None], table, precision=lax.Precision.HIGHEST)

    slots = jnp.arange(orders, dtype=jnp.int32).reshape(lat_count, chan_count, slot_count).transpose(1, 0, 2)
    order_of_place = jnp.take(order_slot, slots.reshape(orders))
    hit = order_of_place[:, None] == jnp.arange(orders, dtype=jnp.int32)[None, :]
    hit = hit.astype(jnp.bfloat16)

    spectrum = jnp.einsum("akc,kn->anc", grid_input, forward, preferred_element_type=jnp.float32)
    spectrum = spectrum.astype(jnp.bfloat16).reshape(lat_dev, 2, orders, channels)
    rows = jnp.einsum("pm,armc->parc", hit, spectrum).astype(jnp.bfloat16)
    rows = rows.reshape(chan_count, group_slots, lat_dev, 2, channels)
    rows = lax.all_to_all(rows, "chan", split_axis=0, concat_axis=0, tiled=True)
    rows = lax.all_gather(rows, "lat", axis=0)
    pairs = lax.all_gather(pairs, "lat", axis=0, tiled=True)

    mixed = jnp.einsum(
        "absurc,bcd->sraud",
        rows,
        mix_weight.reshape(chan_count, channels, -1),
        preferred_element_type=jnp.float32,
    )
    mixed = mixed.reshape(group_slots, 2, latitudes, -1)
    synthesis = jnp.einsum("svt,srtd->vsrd", pairs, mixed, precision=lax.Precision.HIGHEST).astype(jnp.bfloat16)

    synthesis = synthesis.reshape(lat_count, lat_dev, group_slots, 2, -1)
    back = lax.all_to_all(synthesis, "lat", split_axis=0, concat_axis=0, tiled=True)
    back = back.transpose(1, 2, 3, 0, 4).reshape(lat_dev, group_slots, 2, chan_count, channels)
    back = lax.all_to_all(back.transpose(3, 0, 1, 2, 4), "chan", split_axis=0, concat_axis=0, tiled=True)
    back = back.transpose(1, 0, 2, 3, 4).reshape(lat_dev, orders, 2, channels)
    natural = jnp.einsum("pm,aprc->armc", hit, back).astype(jnp.bfloat16)
    field = 2.0 * jnp.einsum(
        "anc,kn->akc",
        natural.reshape(lat_dev, 2 * orders, channels),
        inverse,
        preferred_element_type=jnp.float32,
    )
    return (grid_input.astype(jnp.float32) + jax.nn.gelu(field)).astype(jnp.bfloat16)


def shards(grid_input, legendre, mix_weight, degree_gain, order_slot):
    lat_count, chan_count = lax.axis_size("lat"), lax.axis_size("chan")
    orders, latitudes = order_slot.shape[0], legendre.shape[2]
    compact = (
        lat_count == chan_count == len(STEPS)
        and 2 * latitudes * latitudes == 128
        and orders % (16 * chan_count) == 0
        and grid_input.shape[2] % 128 == 0
        and grid_input.shape[1] % 16 == 0
    )
    body = compact_shards if compact else wide_shards
    return body(grid_input, legendre, mix_weight, degree_gain, order_slot)


def solution(mesh):
    placed = (
        P(("groups", "lat"), None, "chan"),
        P(("lat", "chan"), None, None),
        P(None, "lat"),
        P(),
        P(),
    )
    return jax.shard_map(
        shards,
        mesh=mesh,
        in_specs=placed,
        out_specs=P(("groups", "lat"), None, "chan"),
        check_vma=False,
    )
```

```python
import functools
import math

import jax
import jax.numpy as jnp
import numpy as np
from jax import lax
from jax.experimental import pallas as pl
from jax.experimental.pallas import tpu as pltpu
from jax.sharding import PartitionSpec as P

MIB = 1024 * 1024
PAIR_ROWS = 8
STEPS = (3, 1, 2, 0)
ROOT = math.sqrt(2.0 / math.pi)


def transform_tables(orders, longitudes):
    residue = np.arange(longitudes)[:, None] * np.arange(orders)[None, :] % longitudes
    angle = residue.astype(np.float32) * np.float32(2.0 * math.pi / longitudes)
    scale = np.float32(1.0 / math.sqrt(longitudes))
    forward = np.concatenate([np.cos(angle) * scale, -np.sin(angle) * scale], axis=1)
    weight = np.where(np.arange(2 * orders) % orders == 0, 0.5, 1.0).astype(np.float32)
    return forward.astype(jnp.bfloat16), (forward * weight).astype(jnp.bfloat16)


def grouped_columns(orders, groups):
    return np.arange(2 * orders).reshape(2, groups, orders // groups).transpose(1, 0, 2).reshape(-1)


def analysis_kernel(
    factor, chunk, grid_hbm, table_hbm, legendre_hbm, gain_hbm, slot_hbm, out_ref,
    grid_buf, table_buf, legendre_buf, gain_buf, slot_buf, grid_sem, table_sem, small_sem,
):
    lat_count, chips, _, _ = out_ref.shape
    groups = 2 * chips
    lat_dev, longitudes, channels = grid_buf.shape
    slot_count, latitudes, degrees = legendre_buf.shape
    orders = slot_buf.shape[1]
    group_orders = orders // groups
    group_rows = 2 * group_orders
    chunks = longitudes // chunk
    small = [
        pltpu.make_async_copy(src, dst, small_sem.at[i])
        for i, (src, dst) in enumerate(((legendre_hbm, legendre_buf), (gain_hbm, gain_buf), (slot_hbm, slot_buf)))
    ]
    tables = [pltpu.make_async_copy(table_hbm.at[k], table_buf.at[k], table_sem.at[k]) for k in range(chunks)]
    parts = [
        [
            pltpu.make_async_copy(
                grid_hbm.at[t, pl.ds(k * chunk, chunk)], grid_buf.at[t, pl.ds(k * chunk, chunk)], grid_sem.at[t, k]
            )
            for k in range(chunks)
        ]
        for t in range(lat_dev)
    ]
    for copy in small:
        copy.start()
    for k in range(chunks):
        tables[k].start()
        parts[0][k].start()
    for t in range(1, lat_dev):
        for k in range(chunks):
            parts[t][k].start()

    for copy in small:
        copy.wait()
    lanes = 2 * latitudes * latitudes
    own = (lax.axis_index("lat") * lax.axis_size("chan") + lax.axis_index("chan")) * slot_count
    block = lax.broadcasted_iota(jnp.int32, (1, degrees), 1) // 64
    high_lane = lax.broadcasted_iota(jnp.int32, (1, lanes), 1) < lanes // 2
    sums = []
    for s in range(slot_count):
        rows = legendre_buf[s].astype(jnp.float32)
        weights = jnp.where(block >= slot_buf[0, own + s] // 64, gain_buf[...] * factor, 0.0)
        weighted = rows * weights
        terms = jnp.concatenate([weighted * rows[v : v + 1] for v in range(latitudes)], axis=0)
        sums += [sum(terms[:, k : k + 128] for k in range(0, degrees, 128))] * 2
    sums = jnp.concatenate(sums, axis=0)
    high = sums.astype(jnp.bfloat16)
    low = (sums - high.astype(jnp.float32)).astype(jnp.bfloat16)
    pairs = lax.dot_general(
        jnp.ones((8, 256), jnp.bfloat16),
        jnp.concatenate([high, low], axis=1),
        (((1,), (1,)), ((), ())),
        preferred_element_type=jnp.float32,
    )
    pairs = jnp.concatenate([pairs[:1, s * lanes : (s + 1) * lanes] for s in range(slot_count)], axis=0)
    high = pairs.astype(jnp.bfloat16).astype(jnp.float32)
    pairs = jnp.where(high_lane, high, pairs - high)
    pairs = jnp.concatenate([pairs, jnp.zeros((PAIR_ROWS - slot_count, lanes), jnp.float32)], axis=0)
    pairs = pairs.astype(jnp.bfloat16)
    top = lat_dev * group_rows * (channels // 128)
    for a in range(lat_count):
        for x in range(chips):
            out_ref[a, x, top : top + PAIR_ROWS] = pairs

    for t in range(lat_dev):
        total = None
        for k in range(chunks):
            if t == 0:
                tables[k].wait()
            parts[t][k].wait()
            term = jnp.dot(
                table_buf[k], grid_buf[t, k * chunk : (k + 1) * chunk, :], preferred_element_type=jnp.float32
            )
            total = term if total is None else total + term
        spectrum = total.astype(jnp.bfloat16)
        for g in range(groups):
            for h in range(channels // 128):
                value = spectrum[g * group_rows : (g + 1) * group_rows, h * 128 : (h + 1) * 128]
                at = (h * lat_dev + t) * group_rows
                for a in range(g // chips, lat_count, 2):
                    out_ref[a, g % chips, at : at + group_rows] = value


def mixing_helpers(latitudes, group_orders):
    row = np.arange(latitudes * 2 * group_orders)
    t, rm = row // (2 * group_orders), row % (2 * group_orders)
    lane = np.arange(2 * latitudes * latitudes)
    part, lane_v, lane_t = lane // latitudes**2, lane // latitudes % latitudes, lane % latitudes
    keep = t[:, None] == lane_v[None, :]
    spread = lane_t[:, None] == t[None, :]
    halves = np.concatenate([spread & (part == 0)[:, None], spread & (part == 1)[:, None]], axis=1)
    same = rm[:, None] == rm[None, :]
    return [m.astype(jnp.bfloat16) for m in (keep, halves, same)]


def slot_columns(lat_count, chips, slot_count):
    lat, chip, row = np.indices((lat_count, chips, PAIR_ROWS)).reshape(3, -1)
    slots = np.arange(lat_count * 2 * chips * slot_count)[:, None]
    return np.stack(
        [
            (slots == ((lat * chips + chip) * 2 + core) * slot_count + row) & (row < slot_count)
            for core in range(2)
        ]
    ).astype(jnp.bfloat16)


def choose_kernel(weight_ref, moved_ref, out_ref):
    own = lax.rem(lax.axis_index("lat") + lax.axis_index("chan"), 2) == 0

    @pl.when(own)
    def _():
        out_ref[...] = weight_ref[...]

    @pl.when(jnp.logical_not(own))
    def _():
        out_ref[...] = moved_ref[...]


def channel_products(rows_ref, weight_ref, sender, hit, count):
    lat_count, chips, block_rows, _ = rows_ref.shape
    part_rows = count // lat_count
    channels = weight_ref.shape[0] // (2 * chips)
    split = channels // 128
    mixed = None
    for x in range(chips):
        block = jnp.concatenate(
            [rows_ref[:, x, h * part_rows : (h + 1) * part_rows, :].reshape(count, 128) for h in range(split)], axis=1
        )
        at = pl.ds(pl.multiple_of((2 * x + sender) * channels, channels), channels)
        term = jnp.dot(block, weight_ref[at, :], preferred_element_type=jnp.float32)
        mixed = term if mixed is None else mixed + term
    sent = [
        rows_ref[a, x, split * part_rows :, :].astype(jnp.float32) for a in range(lat_count) for x in range(chips)
    ]
    sent = jnp.concatenate(sent, axis=0).astype(jnp.bfloat16)
    return mixed, jnp.dot(hit, sent, preferred_element_type=jnp.float32)


def first_half_kernel(rows_ref, weight_ref, order_ref, columns_ref, mixed_ref, pairs_ref, hit_ref):
    group_orders = pairs_ref.shape[0]
    chips = rows_ref.shape[1]
    core = lax.rem(lax.axis_index("chan"), 2)
    group = lax.rem(lax.axis_index("lat"), 2) * chips + lax.axis_index("chan") // 2
    orders = jnp.broadcast_to(order_ref[...].astype(jnp.float32), (8, order_ref.shape[1])).astype(jnp.bfloat16)
    hits = []
    for sender in (core, 1 - core):
        order = jnp.dot(orders, columns_ref[sender], preferred_element_type=jnp.float32)[:1].astype(jnp.int32)
        place = lax.broadcasted_iota(jnp.int32, (group_orders, order.shape[1]), 0) + group * group_orders
        hits.append(jnp.where(place == order, 1.0, 0.0).astype(jnp.bfloat16))
    mixed_ref[...], pairs_ref[...] = channel_products(rows_ref, weight_ref, core, hits[0], mixed_ref.shape[0])
    hit_ref[...] = hits[1]


def mixing_kernel(
    mixed_ref, pairs_ref, hit_ref, rows_ref, weight_ref, keep_ref, halves_ref, same_ref, *out_and_scratch
):
    outs, held = out_and_scratch[:-1], out_and_scratch[-1]
    lat_count = rows_ref.shape[0]
    count = same_ref.shape[0]
    group_orders = pairs_ref.shape[0]
    core = lax.rem(lax.axis_index("chan"), 2)
    mixed, pairs = channel_products(rows_ref, weight_ref, 1 - core, hit_ref[...], count)
    mixed = mixed_ref[...] + mixed
    pairs = pairs_ref[...] + pairs
    wide = jnp.concatenate([pairs] * (count // group_orders), axis=0) * keep_ref[...].astype(jnp.float32)
    matrix = jnp.dot(wide.astype(jnp.bfloat16), halves_ref[...], preferred_element_type=jnp.float32)
    same = same_ref[...].astype(jnp.float32)
    high = (matrix[:, :count] * same).astype(jnp.bfloat16)
    low = (matrix[:, count:] * same).astype(jnp.bfloat16)
    mixed_high = mixed.astype(jnp.bfloat16)
    mixed_low = (mixed - mixed_high.astype(jnp.float32)).astype(jnp.bfloat16)
    synthesis = (
        jnp.dot(high, mixed_high, preferred_element_type=jnp.float32)
        + jnp.dot(high, mixed_low, preferred_element_type=jnp.float32)
        + jnp.dot(low, mixed_high, preferred_element_type=jnp.float32)
    )
    held[...] = synthesis.astype(jnp.bfloat16).reshape(held.shape)
    place = lax.axis_index("chan") - core + lax.rem(lax.axis_index("lat"), 2)
    for step, out_ref in zip(STEPS, outs):
        out_ref[...] = held[place ^ step]


def synthesis_kernel(piece, *refs):
    received = refs[:-6]
    grid_ref, table_ref, out_hbm, held, out_buf, out_sem = refs[-6:]
    lat_dev, longitudes, channels = grid_ref.shape
    groups, part_rows, _ = held.shape
    group_rows = part_rows // lat_dev
    for step, received_ref in zip(STEPS, received):
        sender = lax.axis_index("lat") ^ step
        held[lax.rem(sender, 2) * (groups // 2) + sender // 2] = received_ref[...]
    parts = out_sem.shape[1]
    size = longitudes // parts
    copies = []
    for t in range(lat_dev):
        rows = held[:, t * group_rows : (t + 1) * group_rows, :].reshape(groups * group_rows, channels)
        for k in range(parts):
            for at in range(k * size, (k + 1) * size, piece):
                half = jnp.dot(table_ref[at : at + piece, :], rows, preferred_element_type=jnp.float32)
                square = half * half
                inner = half * (2.0 * ROOT + (8.0 * ROOT * 0.044715) * square)
                value = grid_ref[t, at : at + piece, :].astype(jnp.float32) + half * (1.0 + jnp.tanh(inner))
                out_buf[t, at : at + piece, :] = value.astype(jnp.bfloat16)
            span = pl.ds(k * size, size)
            copy = pltpu.make_async_copy(out_buf.at[t, span], out_hbm.at[t, span], out_sem.at[t, k])
            copy.start()
            copies.append(copy)
    for copy in copies:
        copy.wait()


def chunk_of(longitudes):
    return max(n for n in range(16, 1441, 16) if longitudes % n == 0)


def compact_shards(grid_input, legendre, mix_weight, degree_gain, order_slot):
    lat_dev, longitudes, channels = grid_input.shape
    orders = order_slot.shape[0]
    slot_count, degrees, latitudes = legendre.shape
    lat_count = lax.axis_size("lat")
    groups = lax.axis_size("chan")
    chips = groups // 2
    group_orders = orders // groups
    group_rows = 2 * group_orders
    part_rows = lat_dev * group_rows
    block_rows = part_rows * (channels // 128) + PAIR_ROWS
    chunk = chunk_of(longitudes)
    chunks = longitudes // chunk
    columns = grouped_columns(orders, groups)
    forward, inverse = (table[:, columns] for table in transform_tables(orders, longitudes))
    forward = np.ascontiguousarray(forward.reshape(chunks, chunk, 2 * orders).transpose(0, 2, 1))
    hbm = pl.BlockSpec(memory_space=pltpu.HBM)

    both = ("lat", "chan")
    places = [(a, b) for a in range(lat_count) for b in range(groups)]
    moved = lax.ppermute(
        mix_weight, both, [(a * groups + b, (a ^ 1) * groups + b) for a, b in places if (a + b) % 2 == 0]
    )

    weight = pl.pallas_call(
        choose_kernel,
        out_shape=jax.ShapeDtypeStruct(mix_weight.shape, jnp.bfloat16),
        cost_estimate=pl.CostEstimate(flops=100000000000, bytes_accessed=100000000, transcendentals=0),
        compiler_params=pltpu.CompilerParams(vmem_limit_bytes=24 * MIB),
    )(mix_weight, moved)

    sent = pl.pallas_call(
        functools.partial(analysis_kernel, math.sqrt(latitudes / degrees), chunk),
        in_specs=[hbm] * 5,
        out_shape=pltpu.VMEM((lat_count, chips, block_rows, 128), jnp.bfloat16),
        scratch_shapes=[
            pltpu.VMEM(grid_input.shape, jnp.bfloat16),
            pltpu.VMEM(forward.shape, jnp.bfloat16),
            pltpu.VMEM((slot_count, latitudes, degrees), jnp.bfloat16),
            pltpu.VMEM((1, degrees), jnp.float32),
            pltpu.SMEM((1, orders), jnp.int32),
            pltpu.SemaphoreType.DMA((lat_dev, chunks)),
            pltpu.SemaphoreType.DMA((chunks,)),
            pltpu.SemaphoreType.DMA((3,)),
        ],
        compiler_params=pltpu.CompilerParams(vmem_limit_bytes=24 * MIB),
    )(
        *(
            pltpu.with_memory_space_constraint(operand, pltpu.HBM)
            for operand in (
                grid_input,
                jnp.asarray(forward),
                jnp.swapaxes(legendre, 1, 2),
                degree_gain.reshape(1, degrees),
                order_slot.reshape(1, orders),
            )
        )
    )
    cores = [[a * groups + 2 * x + k for a in range(lat_count) for x in range(chips)] for k in range(2)]
    own = lax.all_to_all(
        sent.reshape(lat_count * chips, block_rows, 128),
        both,
        split_axis=0,
        concat_axis=0,
        tiled=True,
        axis_index_groups=cores,
    )
    other = lax.ppermute(own, both, [(n, n ^ 1) for n in range(lat_count * groups)])

    helpers = [jnp.asarray(m) for m in mixing_helpers(latitudes, group_orders)]
    columns_here = mix_weight.shape[1]
    own = own.reshape(lat_count, chips, block_rows, 128)
    other = other.reshape(lat_count, chips, block_rows, 128)
    half = pl.pallas_call(
        first_half_kernel,
        out_shape=[
            jax.ShapeDtypeStruct((lat_count * part_rows, columns_here), jnp.float32),
            jax.ShapeDtypeStruct((group_orders, 128), jnp.float32),
            jax.ShapeDtypeStruct((group_orders, lat_count * chips * PAIR_ROWS), jnp.bfloat16),
        ],
        cost_estimate=pl.CostEstimate(
            flops=lat_count * part_rows * mix_weight.size, bytes_accessed=own.size * 2 + mix_weight.size, transcendentals=0
        ),
        compiler_params=pltpu.CompilerParams(vmem_limit_bytes=24 * MIB),
    )(own, weight, order_slot.reshape(1, orders), jnp.asarray(slot_columns(lat_count, chips, slot_count)))
    parts = pl.pallas_call(
        mixing_kernel,
        out_shape=[jax.ShapeDtypeStruct((part_rows, columns_here), jnp.bfloat16)] * lat_count,
        scratch_shapes=[pltpu.VMEM((lat_count, part_rows, columns_here), jnp.bfloat16)],
        compiler_params=pltpu.CompilerParams(vmem_limit_bytes=24 * MIB),
    )(*half, other, weight, *helpers)
    received = []
    for step, part in zip(STEPS, parts):
        pairs = [
            (a * groups + b, ((b // 2 * 2 + a % 2) ^ step) * groups + a // 2 * 2 + b % 2) for a, b in places
        ]
        received.append(lax.ppermute(part, both, pairs))

    whole = pl.BlockSpec(memory_space=pltpu.VMEM)
    return pl.pallas_call(
        functools.partial(synthesis_kernel, 96),
        in_specs=[whole] * (lat_count + 2),
        out_specs=hbm,
        out_shape=jax.ShapeDtypeStruct(grid_input.shape, jnp.bfloat16),
        scratch_shapes=[
            pltpu.VMEM((groups, part_rows, channels), jnp.bfloat16),
            pltpu.VMEM(grid_input.shape, jnp.bfloat16),
            pltpu.SemaphoreType.DMA((lat_dev, 3)),
        ],
        compiler_params=pltpu.CompilerParams(vmem_limit_bytes=24 * MIB),
    )(*received, grid_input, jnp.asarray(inverse))


def wide_shards(grid_input, legendre, mix_weight, degree_gain, order_slot):
    lat_dev, longitudes, channels = grid_input.shape
    orders = order_slot.shape[0]
    slot_count, degrees, latitudes = legendre.shape
    lat_count = lax.axis_size("lat")
    chan_count = lax.axis_size("chan")
    group_slots = lat_count * slot_count
    forward, inverse = (jnp.asarray(table) for table in transform_tables(orders, longitudes))

    own = (lax.axis_index("lat") * chan_count + lax.axis_index("chan")) * slot_count
    first_block = lax.dynamic_slice_in_dim(order_slot, own, slot_count, 0) // 64
    alive = jnp.arange(degrees, dtype=jnp.int32)[None, :] // 64 >= first_block[:, None]
    weights = jnp.where(alive, degree_gain[None, :] * math.sqrt(latitudes / degrees), 0.0)
    table = legendre.astype(jnp.float32)
    pairs = jnp.einsum("slv,slt->svt", table * weights[:, :, None], table, precision=lax.Precision.HIGHEST)

    slots = jnp.arange(orders, dtype=jnp.int32).reshape(lat_count, chan_count, slot_count).transpose(1, 0, 2)
    order_of_place = jnp.take(order_slot, slots.reshape(orders))
    hit = order_of_place[:, None] == jnp.arange(orders, dtype=jnp.int32)[None, :]
    hit = hit.astype(jnp.bfloat16)

    spectrum = jnp.einsum("akc,kn->anc", grid_input, forward, preferred_element_type=jnp.float32)
    spectrum = spectrum.astype(jnp.bfloat16).reshape(lat_dev, 2, orders, channels)
    rows = jnp.einsum("pm,armc->parc", hit, spectrum).astype(jnp.bfloat16)
    rows = rows.reshape(chan_count, group_slots, lat_dev, 2, channels)
    rows = lax.all_to_all(rows, "chan", split_axis=0, concat_axis=0, tiled=True)
    rows = lax.all_gather(rows, "lat", axis=0)
    pairs = lax.all_gather(pairs, "lat", axis=0, tiled=True)

    mixed = jnp.einsum(
        "absurc,bcd->sraud",
        rows,
        mix_weight.reshape(chan_count, channels, -1),
        preferred_element_type=jnp.float32,
    )
    mixed = mixed.reshape(group_slots, 2, latitudes, -1)
    synthesis = jnp.einsum("svt,srtd->vsrd", pairs, mixed, precision=lax.Precision.HIGHEST).astype(jnp.bfloat16)

    synthesis = synthesis.reshape(lat_count, lat_dev, group_slots, 2, -1)
    back = lax.all_to_all(synthesis, "lat", split_axis=0, concat_axis=0, tiled=True)
    back = back.transpose(1, 2, 3, 0, 4).reshape(lat_dev, group_slots, 2, chan_count, channels)
    back = lax.all_to_all(back.transpose(3, 0, 1, 2, 4), "chan", split_axis=0, concat_axis=0, tiled=True)
    back = back.transpose(1, 0, 2, 3, 4).reshape(lat_dev, orders, 2, channels)
    natural = jnp.einsum("pm,aprc->armc", hit, back).astype(jnp.bfloat16)
    field = 2.0 * jnp.einsum(
        "anc,kn->akc",
        natural.reshape(lat_dev, 2 * orders, channels),
        inverse,
        preferred_element_type=jnp.float32,
    )
    return (grid_input.astype(jnp.float32) + jax.nn.gelu(field)).astype(jnp.bfloat16)


def shards(grid_input, legendre, mix_weight, degree_gain, order_slot):
    lat_count, chan_count = lax.axis_size("lat"), lax.axis_size("chan")
    orders, latitudes = order_slot.shape[0], legendre.shape[2]
    compact = (
        lat_count == chan_count == len(STEPS)
        and 2 * latitudes * latitudes == 128
        and orders % (16 * chan_count) == 0
        and orders <= 256
        and legendre.shape[0] <= PAIR_ROWS
        and grid_input.shape[2] % 128 == 0
        and grid_input.shape[1] % 16 == 0
    )
    body = compact_shards if compact else wide_shards
    return body(grid_input, legendre, mix_weight, degree_gain, order_slot)


def solution(mesh):
    placed = (
        P(("groups", "lat"), None, "chan"),
        P(("lat", "chan"), None, None),
        P(None, "lat"),
        P(),
        P(),
    )
    return jax.shard_map(
        shards,
        mesh=mesh,
        in_specs=placed,
        out_specs=P(("groups", "lat"), None, "chan"),
        check_vma=False,
    )
```

```python
import functools
import math

import jax
import jax.numpy as jnp
import numpy as np
from jax import lax
from jax.experimental import pallas as pl
from jax.experimental.pallas import tpu as pltpu
from jax.sharding import PartitionSpec as P

MIB = 1024 * 1024
PAIR_ROWS = 8
MEMBERS = ((0, 2, 4, 6, 1, 3, 5, 7), (5, 7, 1, 3, 4, 6, 0, 2))
STEPS = (3, 1, 2, 0)
ROOT = math.sqrt(2.0 / math.pi)


def transform_tables(orders, longitudes):
    residue = np.arange(longitudes)[:, None] * np.arange(orders)[None, :] % longitudes
    angle = residue.astype(np.float32) * np.float32(2.0 * math.pi / longitudes)
    scale = np.float32(1.0 / math.sqrt(longitudes))
    forward = np.concatenate([np.cos(angle) * scale, -np.sin(angle) * scale], axis=1)
    weight = np.where(np.arange(2 * orders) % orders == 0, 0.5, 1.0).astype(np.float32)
    return forward.astype(jnp.bfloat16), (forward * weight).astype(jnp.bfloat16)


def grouped_columns(orders, groups):
    return np.arange(2 * orders).reshape(2, groups, orders // groups).transpose(1, 0, 2).reshape(-1)


def place_of(core, chip):
    return jnp.where(core == 0, MEMBERS[0].index(chip), MEMBERS[1].index(chip))


def analysis_kernel(
    factor, chunk, grid_hbm, table_hbm, legendre_hbm, gain_hbm, slot_hbm, out_ref,
    grid_buf, table_buf, legendre_buf, gain_buf, slot_buf, grid_sem, table_sem, small_sem,
):
    lat_count, chips = lax.axis_size("lat"), lax.axis_size("chan") // 2
    groups = 2 * chips
    core = lax.rem(lax.axis_index("chan"), 2)
    lat_dev, longitudes, channels = grid_buf.shape
    slot_count, latitudes, degrees = legendre_buf.shape
    orders = slot_buf.shape[1]
    group_orders = orders // groups
    group_rows = 2 * group_orders
    chunks = longitudes // chunk
    small = [
        pltpu.make_async_copy(src, dst, small_sem.at[i])
        for i, (src, dst) in enumerate(((legendre_hbm, legendre_buf), (gain_hbm, gain_buf), (slot_hbm, slot_buf)))
    ]
    tables = [pltpu.make_async_copy(table_hbm.at[k], table_buf.at[k], table_sem.at[k]) for k in range(chunks)]
    parts = [
        [
            pltpu.make_async_copy(
                grid_hbm.at[t, pl.ds(k * chunk, chunk)], grid_buf.at[t, pl.ds(k * chunk, chunk)], grid_sem.at[t, k]
            )
            for k in range(chunks)
        ]
        for t in range(lat_dev)
    ]
    for copy in small:
        copy.start()
    for k in range(chunks):
        tables[k].start()
        parts[0][k].start()
    for t in range(1, lat_dev):
        for k in range(chunks):
            parts[t][k].start()

    for copy in small:
        copy.wait()
    lanes = 2 * latitudes * latitudes
    own = (lax.axis_index("lat") * lax.axis_size("chan") + lax.axis_index("chan")) * slot_count
    block = lax.broadcasted_iota(jnp.int32, (1, degrees), 1) // 64
    high_lane = lax.broadcasted_iota(jnp.int32, (1, lanes), 1) < lanes // 2
    sums = []
    for s in range(slot_count):
        rows = legendre_buf[s].astype(jnp.float32)
        weights = jnp.where(block >= slot_buf[0, own + s] // 64, gain_buf[...] * factor, 0.0)
        weighted = rows * weights
        terms = jnp.concatenate([weighted * rows[v : v + 1] for v in range(latitudes)], axis=0)
        sums += [sum(terms[:, k : k + 128] for k in range(0, degrees, 128))] * 2
    sums = jnp.concatenate(sums, axis=0)
    high = sums.astype(jnp.bfloat16)
    low = (sums - high.astype(jnp.float32)).astype(jnp.bfloat16)
    pairs = lax.dot_general(
        jnp.ones((8, 256), jnp.bfloat16),
        jnp.concatenate([high, low], axis=1),
        (((1,), (1,)), ((), ())),
        preferred_element_type=jnp.float32,
    )
    pairs = jnp.concatenate([pairs[:1, s * lanes : (s + 1) * lanes] for s in range(slot_count)], axis=0)
    high = pairs.astype(jnp.bfloat16).astype(jnp.float32)
    pairs = jnp.where(high_lane, high, pairs - high)
    pairs = jnp.concatenate([pairs, jnp.zeros((PAIR_ROWS - slot_count, lanes), jnp.float32)], axis=0)
    pairs = pairs.astype(jnp.bfloat16)
    top = lat_dev * group_rows * (channels // 128)
    for a in range(lat_count):
        for x in range(chips):
            out_ref[place_of(core, a * chips + x), top : top + PAIR_ROWS] = pairs

    for t in range(lat_dev):
        total = None
        for k in range(chunks):
            if t == 0:
                tables[k].wait()
            parts[t][k].wait()
            term = jnp.dot(
                table_buf[k], grid_buf[t, k * chunk : (k + 1) * chunk, :], preferred_element_type=jnp.float32
            )
            total = term if total is None else total + term
        spectrum = total.astype(jnp.bfloat16)
        for g in range(groups):
            for h in range(channels // 128):
                value = spectrum[g * group_rows : (g + 1) * group_rows, h * 128 : (h + 1) * 128]
                at = (h * lat_dev + t) * group_rows
                for a in range(g // chips, lat_count, 2):
                    out_ref[place_of(core, a * chips + g % chips), at : at + group_rows] = value


def mixing_helpers(latitudes, group_orders):
    row = np.arange(latitudes * 2 * group_orders)
    t, rm = row // (2 * group_orders), row % (2 * group_orders)
    lane = np.arange(2 * latitudes * latitudes)
    part, lane_v, lane_t = lane // latitudes**2, lane // latitudes % latitudes, lane % latitudes
    keep = t[:, None] == lane_v[None, :]
    spread = lane_t[:, None] == t[None, :]
    halves = np.concatenate([spread & (part == 0)[:, None], spread & (part == 1)[:, None]], axis=1)
    same = rm[:, None] == rm[None, :]
    return [m.astype(jnp.bfloat16) for m in (keep, halves, same)]


def slot_columns(lat_count, chips, slot_count):
    chip, lat, row = np.indices((chips, lat_count, PAIR_ROWS)).reshape(3, -1)
    slots = np.arange(lat_count * 2 * chips * slot_count)[:, None]
    return np.stack(
        [
            (slots == ((lat * chips + chip) * 2 + core) * slot_count + row) & (row < slot_count)
            for core in range(2)
        ]
    ).astype(jnp.bfloat16)


def choose_kernel(weight_ref, moved_ref, out_ref):
    own = lax.rem(lax.axis_index("lat") + lax.axis_index("chan"), 2) == 0

    @pl.when(own)
    def _():
        out_ref[...] = weight_ref[...]

    @pl.when(jnp.logical_not(own))
    def _():
        out_ref[...] = moved_ref[...]


def channel_products(rows_ref, weight_ref, sender, hit, count):
    lat_count, chips = lax.axis_size("lat"), lax.axis_size("chan") // 2
    part_rows = count // lat_count
    channels = weight_ref.shape[0] // (2 * chips)
    split = channels // 128
    mixed = None
    sent = []
    for x in range(chips):
        parts = [rows_ref[place_of(sender, a * chips + x)] for a in range(lat_count)]
        block = jnp.concatenate(
            [
                jnp.concatenate([part[h * part_rows : (h + 1) * part_rows] for part in parts], axis=0)
                for h in range(split)
            ],
            axis=1,
        )
        at = pl.ds(pl.multiple_of((2 * x + sender) * channels, channels), channels)
        term = jnp.dot(block, weight_ref[at, :], preferred_element_type=jnp.float32)
        mixed = term if mixed is None else mixed + term
        sent += [part[split * part_rows :].astype(jnp.float32) for part in parts]
    sent = jnp.concatenate(sent, axis=0).astype(jnp.bfloat16)
    return mixed, jnp.dot(hit, sent, preferred_element_type=jnp.float32)


def first_half_kernel(rows_ref, weight_ref, order_ref, columns_ref, mixed_ref, pairs_ref, hit_ref):
    group_orders = pairs_ref.shape[0]
    chips = lax.axis_size("chan") // 2
    core = lax.rem(lax.axis_index("chan"), 2)
    group = lax.rem(lax.axis_index("lat"), 2) * chips + lax.axis_index("chan") // 2
    orders = jnp.broadcast_to(order_ref[...].astype(jnp.float32), (8, order_ref.shape[1])).astype(jnp.bfloat16)
    hits = []
    for sender in (core, 1 - core):
        order = jnp.dot(orders, columns_ref[sender], preferred_element_type=jnp.float32)[:1].astype(jnp.int32)
        place = lax.broadcasted_iota(jnp.int32, (group_orders, order.shape[1]), 0) + group * group_orders
        hits.append(jnp.where(place == order, 1.0, 0.0).astype(jnp.bfloat16))
    mixed_ref[...], pairs_ref[...] = channel_products(rows_ref, weight_ref, core, hits[0], mixed_ref.shape[0])
    hit_ref[...] = hits[1]


def mixing_kernel(
    mixed_ref, pairs_ref, hit_ref, rows_ref, weight_ref, keep_ref, halves_ref, same_ref, *out_and_scratch
):
    outs, held = out_and_scratch[:-1], out_and_scratch[-1]
    lat_count = len(outs)
    count = same_ref.shape[0]
    group_orders = pairs_ref.shape[0]
    core = lax.rem(lax.axis_index("chan"), 2)
    mixed, pairs = channel_products(rows_ref, weight_ref, 1 - core, hit_ref[...], count)
    mixed = mixed_ref[...] + mixed
    pairs = pairs_ref[...] + pairs
    wide = jnp.concatenate([pairs] * (count // group_orders), axis=0) * keep_ref[...].astype(jnp.float32)
    matrix = jnp.dot(wide.astype(jnp.bfloat16), halves_ref[...], preferred_element_type=jnp.float32)
    same = same_ref[...].astype(jnp.float32)
    high = (matrix[:, :count] * same).astype(jnp.bfloat16)
    low = (matrix[:, count:] * same).astype(jnp.bfloat16)
    mixed_high = mixed.astype(jnp.bfloat16)
    mixed_low = (mixed - mixed_high.astype(jnp.float32)).astype(jnp.bfloat16)
    synthesis = (
        jnp.dot(high, mixed_high, preferred_element_type=jnp.float32)
        + jnp.dot(high, mixed_low, preferred_element_type=jnp.float32)
        + jnp.dot(low, mixed_high, preferred_element_type=jnp.float32)
    )
    held[...] = synthesis.astype(jnp.bfloat16).reshape(held.shape)
    place = lax.axis_index("chan") - core + lax.rem(lax.axis_index("lat"), 2)
    for step, out_ref in zip(STEPS, outs):
        out_ref[...] = held[place ^ step]


def synthesis_kernel(piece, *refs):
    received = refs[:-6]
    grid_ref, table_ref, out_hbm, held, out_buf, out_sem = refs[-6:]
    lat_dev, longitudes, channels = grid_ref.shape
    groups, part_rows, _ = held.shape
    group_rows = part_rows // lat_dev
    for step, received_ref in zip(STEPS, received):
        sender = lax.axis_index("lat") ^ step
        held[lax.rem(sender, 2) * (groups // 2) + sender // 2] = received_ref[...]
    parts = out_sem.shape[1]
    size = longitudes // parts
    copies = []
    for t in range(lat_dev):
        rows = held[:, t * group_rows : (t + 1) * group_rows, :].reshape(groups * group_rows, channels)
        for k in range(parts):
            for at in range(k * size, (k + 1) * size, piece):
                half = jnp.dot(table_ref[at : at + piece, :], rows, preferred_element_type=jnp.float32)
                square = half * half
                inner = half * (2.0 * ROOT + (8.0 * ROOT * 0.044715) * square)
                value = grid_ref[t, at : at + piece, :].astype(jnp.float32) + half * (1.0 + jnp.tanh(inner))
                out_buf[t, at : at + piece, :] = value.astype(jnp.bfloat16)
            span = pl.ds(k * size, size)
            copy = pltpu.make_async_copy(out_buf.at[t, span], out_hbm.at[t, span], out_sem.at[t, k])
            copy.start()
            copies.append(copy)
    for copy in copies:
        copy.wait()


def chunk_of(longitudes):
    return max(n for n in range(16, 1441, 16) if longitudes % n == 0)


def compact_shards(grid_input, legendre, mix_weight, degree_gain, order_slot):
    lat_dev, longitudes, channels = grid_input.shape
    orders = order_slot.shape[0]
    slot_count, degrees, latitudes = legendre.shape
    lat_count = lax.axis_size("lat")
    groups = lax.axis_size("chan")
    chips = groups // 2
    group_orders = orders // groups
    group_rows = 2 * group_orders
    part_rows = lat_dev * group_rows
    block_rows = part_rows * (channels // 128) + PAIR_ROWS
    chunk = chunk_of(longitudes)
    chunks = longitudes // chunk
    columns = grouped_columns(orders, groups)
    forward, inverse = (table[:, columns] for table in transform_tables(orders, longitudes))
    forward = np.ascontiguousarray(forward.reshape(chunks, chunk, 2 * orders).transpose(0, 2, 1))
    hbm = pl.BlockSpec(memory_space=pltpu.HBM)

    both = ("lat", "chan")
    places = [(a, b) for a in range(lat_count) for b in range(groups)]
    moved = lax.ppermute(
        mix_weight, both, [(a * groups + b, (a ^ 1) * groups + b) for a, b in places if (a + b) % 2 == 0]
    )

    weight = pl.pallas_call(
        choose_kernel,
        out_shape=jax.ShapeDtypeStruct(mix_weight.shape, jnp.bfloat16),
        cost_estimate=pl.CostEstimate(flops=100000000000, bytes_accessed=100000000, transcendentals=0),
        compiler_params=pltpu.CompilerParams(vmem_limit_bytes=24 * MIB),
    )(mix_weight, moved)

    sent = pl.pallas_call(
        functools.partial(analysis_kernel, math.sqrt(latitudes / degrees), chunk),
        in_specs=[hbm] * 5,
        out_shape=pltpu.VMEM((lat_count * chips, block_rows, 128), jnp.bfloat16),
        scratch_shapes=[
            pltpu.VMEM(grid_input.shape, jnp.bfloat16),
            pltpu.VMEM(forward.shape, jnp.bfloat16),
            pltpu.VMEM((slot_count, latitudes, degrees), jnp.bfloat16),
            pltpu.VMEM((1, degrees), jnp.float32),
            pltpu.SMEM((1, orders), jnp.int32),
            pltpu.SemaphoreType.DMA((lat_dev, chunks)),
            pltpu.SemaphoreType.DMA((chunks,)),
            pltpu.SemaphoreType.DMA((3,)),
        ],
        compiler_params=pltpu.CompilerParams(vmem_limit_bytes=24 * MIB),
    )(
        *(
            pltpu.with_memory_space_constraint(operand, pltpu.HBM)
            for operand in (
                grid_input,
                jnp.asarray(forward),
                jnp.swapaxes(legendre, 1, 2),
                degree_gain.reshape(1, degrees),
                order_slot.reshape(1, orders),
            )
        )
    )
    cores = [[n // chips * groups + n % chips * 2 + k for n in MEMBERS[k]] for k in range(2)]
    own = lax.all_to_all(
        sent,
        both,
        split_axis=0,
        concat_axis=0,
        tiled=True,
        axis_index_groups=cores,
    )
    other = lax.ppermute(own, both, [(n, n ^ 1) for n in range(lat_count * groups)])

    helpers = [jnp.asarray(m) for m in mixing_helpers(latitudes, group_orders)]
    columns_here = mix_weight.shape[1]
    half = pl.pallas_call(
        first_half_kernel,
        out_shape=[
            jax.ShapeDtypeStruct((lat_count * part_rows, columns_here), jnp.float32),
            jax.ShapeDtypeStruct((group_orders, 128), jnp.float32),
            jax.ShapeDtypeStruct((group_orders, lat_count * chips * PAIR_ROWS), jnp.bfloat16),
        ],
        cost_estimate=pl.CostEstimate(
            flops=lat_count * part_rows * mix_weight.size, bytes_accessed=own.size * 2 + mix_weight.size, transcendentals=0
        ),
        compiler_params=pltpu.CompilerParams(vmem_limit_bytes=24 * MIB),
    )(own, weight, order_slot.reshape(1, orders), jnp.asarray(slot_columns(lat_count, chips, slot_count)))
    parts = pl.pallas_call(
        mixing_kernel,
        out_shape=[jax.ShapeDtypeStruct((part_rows, columns_here), jnp.bfloat16)] * lat_count,
        scratch_shapes=[pltpu.VMEM((lat_count, part_rows, columns_here), jnp.bfloat16)],
        compiler_params=pltpu.CompilerParams(vmem_limit_bytes=24 * MIB),
    )(*half, other, weight, *helpers)
    received = []
    for step, part in zip(STEPS, parts):
        pairs = [
            (a * groups + b, ((b // 2 * 2 + a % 2) ^ step) * groups + a // 2 * 2 + b % 2) for a, b in places
        ]
        received.append(lax.ppermute(part, both, pairs))

    whole = pl.BlockSpec(memory_space=pltpu.VMEM)
    return pl.pallas_call(
        functools.partial(synthesis_kernel, 96),
        in_specs=[whole] * (lat_count + 2),
        out_specs=hbm,
        out_shape=jax.ShapeDtypeStruct(grid_input.shape, jnp.bfloat16),
        scratch_shapes=[
            pltpu.VMEM((groups, part_rows, channels), jnp.bfloat16),
            pltpu.VMEM(grid_input.shape, jnp.bfloat16),
            pltpu.SemaphoreType.DMA((lat_dev, 3)),
        ],
        compiler_params=pltpu.CompilerParams(vmem_limit_bytes=24 * MIB),
    )(*received, grid_input, jnp.asarray(inverse))


def wide_shards(grid_input, legendre, mix_weight, degree_gain, order_slot):
    lat_dev, longitudes, channels = grid_input.shape
    orders = order_slot.shape[0]
    slot_count, degrees, latitudes = legendre.shape
    lat_count = lax.axis_size("lat")
    chan_count = lax.axis_size("chan")
    group_slots = lat_count * slot_count
    forward, inverse = (jnp.asarray(table) for table in transform_tables(orders, longitudes))

    own = (lax.axis_index("lat") * chan_count + lax.axis_index("chan")) * slot_count
    first_block = lax.dynamic_slice_in_dim(order_slot, own, slot_count, 0) // 64
    alive = jnp.arange(degrees, dtype=jnp.int32)[None, :] // 64 >= first_block[:, None]
    weights = jnp.where(alive, degree_gain[None, :] * math.sqrt(latitudes / degrees), 0.0)
    table = legendre.astype(jnp.float32)
    pairs = jnp.einsum("slv,slt->svt", table * weights[:, :, None], table, precision=lax.Precision.HIGHEST)

    slots = jnp.arange(orders, dtype=jnp.int32).reshape(lat_count, chan_count, slot_count).transpose(1, 0, 2)
    order_of_place = jnp.take(order_slot, slots.reshape(orders))
    hit = order_of_place[:, None] == jnp.arange(orders, dtype=jnp.int32)[None, :]
    hit = hit.astype(jnp.bfloat16)

    spectrum = jnp.einsum("akc,kn->anc", grid_input, forward, preferred_element_type=jnp.float32)
    spectrum = spectrum.astype(jnp.bfloat16).reshape(lat_dev, 2, orders, channels)
    rows = jnp.einsum("pm,armc->parc", hit, spectrum).astype(jnp.bfloat16)
    rows = rows.reshape(chan_count, group_slots, lat_dev, 2, channels)
    rows = lax.all_to_all(rows, "chan", split_axis=0, concat_axis=0, tiled=True)
    rows = lax.all_gather(rows, "lat", axis=0)
    pairs = lax.all_gather(pairs, "lat", axis=0, tiled=True)

    mixed = jnp.einsum(
        "absurc,bcd->sraud",
        rows,
        mix_weight.reshape(chan_count, channels, -1),
        preferred_element_type=jnp.float32,
    )
    mixed = mixed.reshape(group_slots, 2, latitudes, -1)
    synthesis = jnp.einsum("svt,srtd->vsrd", pairs, mixed, precision=lax.Precision.HIGHEST).astype(jnp.bfloat16)

    synthesis = synthesis.reshape(lat_count, lat_dev, group_slots, 2, -1)
    back = lax.all_to_all(synthesis, "lat", split_axis=0, concat_axis=0, tiled=True)
    back = back.transpose(1, 2, 3, 0, 4).reshape(lat_dev, group_slots, 2, chan_count, channels)
    back = lax.all_to_all(back.transpose(3, 0, 1, 2, 4), "chan", split_axis=0, concat_axis=0, tiled=True)
    back = back.transpose(1, 0, 2, 3, 4).reshape(lat_dev, orders, 2, channels)
    natural = jnp.einsum("pm,aprc->armc", hit, back).astype(jnp.bfloat16)
    field = 2.0 * jnp.einsum(
        "anc,kn->akc",
        natural.reshape(lat_dev, 2 * orders, channels),
        inverse,
        preferred_element_type=jnp.float32,
    )
    return (grid_input.astype(jnp.float32) + jax.nn.gelu(field)).astype(jnp.bfloat16)


def shards(grid_input, legendre, mix_weight, degree_gain, order_slot):
    lat_count, chan_count = lax.axis_size("lat"), lax.axis_size("chan")
    orders, latitudes = order_slot.shape[0], legendre.shape[2]
    compact = (
        lat_count == chan_count == len(STEPS) == len(MEMBERS[0]) // 2
        and 2 * latitudes * latitudes == 128
        and orders % (16 * chan_count) == 0
        and orders <= 256
        and legendre.shape[0] <= PAIR_ROWS
        and grid_input.shape[2] % 128 == 0
        and grid_input.shape[1] % 16 == 0
    )
    body = compact_shards if compact else wide_shards
    return body(grid_input, legendre, mix_weight, degree_gain, order_slot)


def solution(mesh):
    placed = (
        P(("groups", "lat"), None, "chan"),
        P(("lat", "chan"), None, None),
        P(None, "lat"),
        P(),
        P(),
    )
    return jax.shard_map(
        shards,
        mesh=mesh,
        in_specs=placed,
        out_specs=P(("groups", "lat"), None, "chan"),
        check_vma=False,
    )
```

```python
import functools
import math

import jax
import jax.numpy as jnp
import numpy as np
from jax import lax
from jax.experimental import pallas as pl
from jax.experimental.pallas import tpu as pltpu
from jax.sharding import PartitionSpec as P

MIB = 1024 * 1024
PAIR_ROWS = 8
MEMBERS = ((0, 2, 4, 6, 1, 3, 5, 7), (5, 7, 1, 3, 4, 6, 0, 2))
STEPS = (3, 1, 2, 0)
ROOT = math.sqrt(2.0 / math.pi)


def transform_tables(orders, longitudes):
    residue = np.arange(longitudes)[:, None] * np.arange(orders)[None, :] % longitudes
    angle = residue.astype(np.float32) * np.float32(2.0 * math.pi / longitudes)
    scale = np.float32(1.0 / math.sqrt(longitudes))
    forward = np.concatenate([np.cos(angle) * scale, -np.sin(angle) * scale], axis=1)
    weight = np.where(np.arange(2 * orders) % orders == 0, 0.5, 1.0).astype(np.float32)
    return forward.astype(jnp.bfloat16), (forward * weight).astype(jnp.bfloat16)


def grouped_columns(orders, groups):
    return np.arange(2 * orders).reshape(2, groups, orders // groups).transpose(1, 0, 2).reshape(-1)


def place_of(core, chip):
    return jnp.where(core == 0, MEMBERS[0].index(chip), MEMBERS[1].index(chip))


def analysis_kernel(
    factor, chunk, grid_hbm, table_hbm, legendre_hbm, gain_hbm, slot_hbm, out_ref,
    grid_buf, table_buf, legendre_buf, gain_buf, slot_buf, grid_sem, table_sem, small_sem,
):
    lat_count, chips = lax.axis_size("lat"), lax.axis_size("chan") // 2
    groups = 2 * chips
    core = lax.rem(lax.axis_index("chan"), 2)
    lat_dev, longitudes, channels = grid_buf.shape
    slot_count, latitudes, degrees = legendre_buf.shape
    orders = slot_buf.shape[1]
    group_orders = orders // groups
    group_rows = 2 * group_orders
    chunks = longitudes // chunk
    small = [
        pltpu.make_async_copy(src, dst, small_sem.at[i])
        for i, (src, dst) in enumerate(((legendre_hbm, legendre_buf), (gain_hbm, gain_buf), (slot_hbm, slot_buf)))
    ]
    tables = [pltpu.make_async_copy(table_hbm.at[k], table_buf.at[k], table_sem.at[k]) for k in range(chunks)]
    parts = [
        [
            pltpu.make_async_copy(
                grid_hbm.at[t, pl.ds(k * chunk, chunk)], grid_buf.at[t, pl.ds(k * chunk, chunk)], grid_sem.at[t, k]
            )
            for k in range(chunks)
        ]
        for t in range(lat_dev)
    ]
    for copy in small:
        copy.start()
    for k in range(chunks):
        tables[k].start(priority=1)
        parts[0][k].start()
    for t in range(1, lat_dev):
        for k in range(chunks):
            parts[t][k].start(priority=1)

    for copy in small:
        copy.wait()
    lanes = 2 * latitudes * latitudes
    own = (lax.axis_index("lat") * lax.axis_size("chan") + lax.axis_index("chan")) * slot_count
    block = lax.broadcasted_iota(jnp.int32, (1, degrees), 1) // 64
    high_lane = lax.broadcasted_iota(jnp.int32, (1, lanes), 1) < lanes // 2
    sums = []
    for s in range(slot_count):
        rows = legendre_buf[s].astype(jnp.float32)
        weights = jnp.where(block >= slot_buf[0, own + s] // 64, gain_buf[...] * factor, 0.0)
        weighted = rows * weights
        terms = jnp.concatenate([weighted * rows[v : v + 1] for v in range(latitudes)], axis=0)
        sums += [sum(terms[:, k : k + 128] for k in range(0, degrees, 128))] * 2
    sums = jnp.concatenate(sums, axis=0)
    high = sums.astype(jnp.bfloat16)
    low = (sums - high.astype(jnp.float32)).astype(jnp.bfloat16)
    pairs = lax.dot_general(
        jnp.ones((8, 256), jnp.bfloat16),
        jnp.concatenate([high, low], axis=1),
        (((1,), (1,)), ((), ())),
        preferred_element_type=jnp.float32,
    )
    pairs = jnp.concatenate([pairs[:1, s * lanes : (s + 1) * lanes] for s in range(slot_count)], axis=0)
    high = pairs.astype(jnp.bfloat16).astype(jnp.float32)
    pairs = jnp.where(high_lane, high, pairs - high)
    pairs = jnp.concatenate([pairs, jnp.zeros((PAIR_ROWS - slot_count, lanes), jnp.float32)], axis=0)
    pairs = pairs.astype(jnp.bfloat16)
    top = lat_dev * group_rows * (channels // 128)
    for a in range(lat_count):
        for x in range(chips):
            out_ref[place_of(core, a * chips + x), top : top + PAIR_ROWS] = pairs

    for t in range(lat_dev):
        total = None
        for k in range(chunks):
            if t == 0:
                tables[k].wait()
            parts[t][k].wait()
            term = jnp.dot(
                table_buf[k], grid_buf[t, k * chunk : (k + 1) * chunk, :], preferred_element_type=jnp.float32
            )
            total = term if total is None else total + term
        spectrum = total.astype(jnp.bfloat16)
        for g in range(groups):
            for h in range(channels // 128):
                value = spectrum[g * group_rows : (g + 1) * group_rows, h * 128 : (h + 1) * 128]
                at = (h * lat_dev + t) * group_rows
                for a in range(g // chips, lat_count, 2):
                    out_ref[place_of(core, a * chips + g % chips), at : at + group_rows] = value


def mixing_helpers(latitudes, group_orders):
    row = np.arange(latitudes * 2 * group_orders)
    t, rm = row // (2 * group_orders), row % (2 * group_orders)
    lane = np.arange(2 * latitudes * latitudes)
    part, lane_v, lane_t = lane // latitudes**2, lane // latitudes % latitudes, lane % latitudes
    keep = t[:, None] == lane_v[None, :]
    spread = lane_t[:, None] == t[None, :]
    halves = np.concatenate([spread & (part == 0)[:, None], spread & (part == 1)[:, None]], axis=1)
    same = rm[:, None] == rm[None, :]
    return [m.astype(jnp.bfloat16) for m in (keep, halves, same)]


def slot_columns(lat_count, chips, slot_count):
    chip, lat, row = np.indices((chips, lat_count, PAIR_ROWS)).reshape(3, -1)
    slots = np.arange(lat_count * 2 * chips * slot_count)[:, None]
    return np.stack(
        [
            (slots == ((lat * chips + chip) * 2 + core) * slot_count + row) & (row < slot_count)
            for core in range(2)
        ]
    ).astype(jnp.bfloat16)


def choose_kernel(weight_ref, moved_ref, out_ref):
    own = lax.rem(lax.axis_index("lat") + lax.axis_index("chan"), 2) == 0

    @pl.when(own)
    def _():
        out_ref[...] = weight_ref[...]

    @pl.when(jnp.logical_not(own))
    def _():
        out_ref[...] = moved_ref[...]


def channel_products(rows_ref, weight_ref, sender, hit, count):
    lat_count, chips = lax.axis_size("lat"), lax.axis_size("chan") // 2
    part_rows = count // lat_count
    channels = weight_ref.shape[0] // (2 * chips)
    split = channels // 128
    mixed = None
    sent = []
    for x in range(chips):
        parts = [rows_ref[place_of(sender, a * chips + x)] for a in range(lat_count)]
        block = jnp.concatenate(
            [
                jnp.concatenate([part[h * part_rows : (h + 1) * part_rows] for part in parts], axis=0)
                for h in range(split)
            ],
            axis=1,
        )
        at = pl.ds(pl.multiple_of((2 * x + sender) * channels, channels), channels)
        term = jnp.dot(block, weight_ref[at, :], preferred_element_type=jnp.float32)
        mixed = term if mixed is None else mixed + term
        sent += [part[split * part_rows :].astype(jnp.float32) for part in parts]
    sent = jnp.concatenate(sent, axis=0).astype(jnp.bfloat16)
    return mixed, jnp.dot(hit, sent, preferred_element_type=jnp.float32)


def first_half_kernel(rows_ref, weight_ref, order_ref, columns_ref, mixed_ref, pairs_ref, hit_ref):
    group_orders = pairs_ref.shape[0]
    chips = lax.axis_size("chan") // 2
    core = lax.rem(lax.axis_index("chan"), 2)
    group = lax.rem(lax.axis_index("lat"), 2) * chips + lax.axis_index("chan") // 2
    orders = jnp.broadcast_to(order_ref[...].astype(jnp.float32), (8, order_ref.shape[1])).astype(jnp.bfloat16)
    hits = []
    for sender in (core, 1 - core):
        order = jnp.dot(orders, columns_ref[sender], preferred_element_type=jnp.float32)[:1].astype(jnp.int32)
        place = lax.broadcasted_iota(jnp.int32, (group_orders, order.shape[1]), 0) + group * group_orders
        hits.append(jnp.where(place == order, 1.0, 0.0).astype(jnp.bfloat16))
    mixed_ref[...], pairs_ref[...] = channel_products(rows_ref, weight_ref, core, hits[0], mixed_ref.shape[0])
    hit_ref[...] = hits[1]


def mixing_kernel(
    mixed_ref, pairs_ref, hit_ref, rows_ref, weight_ref, keep_ref, halves_ref, same_ref, *out_and_scratch
):
    outs, held = out_and_scratch[:-1], out_and_scratch[-1]
    lat_count = len(outs)
    count = same_ref.shape[0]
    group_orders = pairs_ref.shape[0]
    core = lax.rem(lax.axis_index("chan"), 2)
    mixed, pairs = channel_products(rows_ref, weight_ref, 1 - core, hit_ref[...], count)
    mixed = mixed_ref[...] + mixed
    pairs = pairs_ref[...] + pairs
    wide = jnp.concatenate([pairs.astype(jnp.bfloat16)] * (count // group_orders), axis=0) * keep_ref[...]
    matrix = jnp.dot(wide, halves_ref[...], preferred_element_type=jnp.float32).astype(jnp.bfloat16)
    same = same_ref[...]
    high, low = matrix[:, :count] * same, matrix[:, count:] * same
    mixed_high = mixed.astype(jnp.bfloat16)
    mixed_low = (mixed - mixed_high.astype(jnp.float32)).astype(jnp.bfloat16)
    synthesis = jnp.dot(
        jnp.concatenate([high, high, low], axis=1),
        jnp.concatenate([mixed_high, mixed_low, mixed_high], axis=0),
        preferred_element_type=jnp.float32,
    )
    held[...] = synthesis.astype(jnp.bfloat16).reshape(held.shape)
    place = lax.axis_index("chan") - core + lax.rem(lax.axis_index("lat"), 2)
    for step, out_ref in zip(STEPS, outs):
        out_ref[...] = held[place ^ step]


def synthesis_kernel(piece, *refs):
    received = refs[:-6]
    grid_ref, table_ref, out_hbm, held, out_buf, out_sem = refs[-6:]
    lat_dev, longitudes, channels = grid_ref.shape
    groups, part_rows, _ = held.shape
    group_rows = part_rows // lat_dev
    for step, received_ref in zip(STEPS, received):
        sender = lax.axis_index("lat") ^ step
        held[lax.rem(sender, 2) * (groups // 2) + sender // 2] = received_ref[...]
    parts = out_sem.shape[1]
    size = longitudes // parts
    copies = []
    for t in range(lat_dev):
        rows = held[:, t * group_rows : (t + 1) * group_rows, :].reshape(groups * group_rows, channels)
        for k in range(parts):
            for at in range(k * size, (k + 1) * size, piece):
                half = jnp.dot(table_ref[at : at + piece, :], rows, preferred_element_type=jnp.float32)
                square = half * half
                inner = half * (2.0 * ROOT + (8.0 * ROOT * 0.044715) * square)
                value = grid_ref[t, at : at + piece, :].astype(jnp.float32) + half * (1.0 + jnp.tanh(inner))
                out_buf[t, at : at + piece, :] = value.astype(jnp.bfloat16)
            span = pl.ds(k * size, size)
            copy = pltpu.make_async_copy(out_buf.at[t, span], out_hbm.at[t, span], out_sem.at[t, k])
            copy.start(priority=t % 2)
            copies.append(copy)
    for copy in copies:
        copy.wait()


def chunk_of(longitudes):
    return max(n for n in range(16, 1441, 16) if longitudes % n == 0)


def compact_shards(grid_input, legendre, mix_weight, degree_gain, order_slot):
    lat_dev, longitudes, channels = grid_input.shape
    orders = order_slot.shape[0]
    slot_count, degrees, latitudes = legendre.shape
    lat_count = lax.axis_size("lat")
    groups = lax.axis_size("chan")
    chips = groups // 2
    group_orders = orders // groups
    group_rows = 2 * group_orders
    part_rows = lat_dev * group_rows
    block_rows = part_rows * (channels // 128) + PAIR_ROWS
    chunk = chunk_of(longitudes)
    chunks = longitudes // chunk
    columns = grouped_columns(orders, groups)
    forward, inverse = (table[:, columns] for table in transform_tables(orders, longitudes))
    forward = np.ascontiguousarray(forward.reshape(chunks, chunk, 2 * orders).transpose(0, 2, 1))
    hbm = pl.BlockSpec(memory_space=pltpu.HBM)

    both = ("lat", "chan")
    places = [(a, b) for a in range(lat_count) for b in range(groups)]
    moved = lax.ppermute(
        mix_weight, both, [(a * groups + b, (a ^ 1) * groups + b) for a, b in places if (a + b) % 2 == 0]
    )

    weight = pl.pallas_call(
        choose_kernel,
        out_shape=jax.ShapeDtypeStruct(mix_weight.shape, jnp.bfloat16),
        cost_estimate=pl.CostEstimate(flops=100000000000, bytes_accessed=100000000, transcendentals=0),
        compiler_params=pltpu.CompilerParams(vmem_limit_bytes=24 * MIB),
    )(mix_weight, moved)

    sent = pl.pallas_call(
        functools.partial(analysis_kernel, math.sqrt(latitudes / degrees), chunk),
        in_specs=[hbm] * 5,
        out_shape=pltpu.VMEM((lat_count * chips, block_rows, 128), jnp.bfloat16),
        scratch_shapes=[
            pltpu.VMEM(grid_input.shape, jnp.bfloat16),
            pltpu.VMEM(forward.shape, jnp.bfloat16),
            pltpu.VMEM((slot_count, latitudes, degrees), jnp.bfloat16),
            pltpu.VMEM((1, degrees), jnp.float32),
            pltpu.SMEM((1, orders), jnp.int32),
            pltpu.SemaphoreType.DMA((lat_dev, chunks)),
            pltpu.SemaphoreType.DMA((chunks,)),
            pltpu.SemaphoreType.DMA((3,)),
        ],
        compiler_params=pltpu.CompilerParams(vmem_limit_bytes=24 * MIB),
    )(
        *(
            pltpu.with_memory_space_constraint(operand, pltpu.HBM)
            for operand in (
                grid_input,
                jnp.asarray(forward),
                jnp.swapaxes(legendre, 1, 2),
                degree_gain.reshape(1, degrees),
                order_slot.reshape(1, orders),
            )
        )
    )
    cores = [[n // chips * groups + n % chips * 2 + k for n in MEMBERS[k]] for k in range(2)]
    own = lax.all_to_all(
        sent,
        both,
        split_axis=0,
        concat_axis=0,
        tiled=True,
        axis_index_groups=cores,
    )
    other = lax.ppermute(own, both, [(n, n ^ 1) for n in range(lat_count * groups)])

    helpers = [jnp.asarray(m) for m in mixing_helpers(latitudes, group_orders)]
    columns_here = mix_weight.shape[1]
    half = pl.pallas_call(
        first_half_kernel,
        out_shape=[
            jax.ShapeDtypeStruct((lat_count * part_rows, columns_here), jnp.float32),
            jax.ShapeDtypeStruct((group_orders, 128), jnp.float32),
            jax.ShapeDtypeStruct((group_orders, lat_count * chips * PAIR_ROWS), jnp.bfloat16),
        ],
        cost_estimate=pl.CostEstimate(
            flops=lat_count * part_rows * mix_weight.size, bytes_accessed=own.size * 2 + mix_weight.size, transcendentals=0
        ),
        compiler_params=pltpu.CompilerParams(vmem_limit_bytes=24 * MIB),
    )(own, weight, order_slot.reshape(1, orders), jnp.asarray(slot_columns(lat_count, chips, slot_count)))
    parts = pl.pallas_call(
        mixing_kernel,
        out_shape=[jax.ShapeDtypeStruct((part_rows, columns_here), jnp.bfloat16)] * lat_count,
        scratch_shapes=[pltpu.VMEM((lat_count, part_rows, columns_here), jnp.bfloat16)],
        compiler_params=pltpu.CompilerParams(vmem_limit_bytes=24 * MIB),
    )(*half, other, weight, *helpers)
    received = []
    for step, part in zip(STEPS, parts):
        pairs = [
            (a * groups + b, ((b // 2 * 2 + a % 2) ^ step) * groups + a // 2 * 2 + b % 2) for a, b in places
        ]
        received.append(lax.ppermute(part, both, pairs))

    whole = pl.BlockSpec(memory_space=pltpu.VMEM)
    return pl.pallas_call(
        functools.partial(synthesis_kernel, 96),
        in_specs=[whole] * (lat_count + 2),
        out_specs=hbm,
        out_shape=jax.ShapeDtypeStruct(grid_input.shape, jnp.bfloat16),
        scratch_shapes=[
            pltpu.VMEM((groups, part_rows, channels), jnp.bfloat16),
            pltpu.VMEM(grid_input.shape, jnp.bfloat16),
            pltpu.SemaphoreType.DMA((lat_dev, 3)),
        ],
        compiler_params=pltpu.CompilerParams(vmem_limit_bytes=24 * MIB),
    )(*received, grid_input, jnp.asarray(inverse))


def wide_shards(grid_input, legendre, mix_weight, degree_gain, order_slot):
    lat_dev, longitudes, channels = grid_input.shape
    orders = order_slot.shape[0]
    slot_count, degrees, latitudes = legendre.shape
    lat_count = lax.axis_size("lat")
    chan_count = lax.axis_size("chan")
    group_slots = lat_count * slot_count
    forward, inverse = (jnp.asarray(table) for table in transform_tables(orders, longitudes))

    own = (lax.axis_index("lat") * chan_count + lax.axis_index("chan")) * slot_count
    first_block = lax.dynamic_slice_in_dim(order_slot, own, slot_count, 0) // 64
    alive = jnp.arange(degrees, dtype=jnp.int32)[None, :] // 64 >= first_block[:, None]
    weights = jnp.where(alive, degree_gain[None, :] * math.sqrt(latitudes / degrees), 0.0)
    table = legendre.astype(jnp.float32)
    pairs = jnp.einsum("slv,slt->svt", table * weights[:, :, None], table, precision=lax.Precision.HIGHEST)

    slots = jnp.arange(orders, dtype=jnp.int32).reshape(lat_count, chan_count, slot_count).transpose(1, 0, 2)
    order_of_place = jnp.take(order_slot, slots.reshape(orders))
    hit = order_of_place[:, None] == jnp.arange(orders, dtype=jnp.int32)[None, :]
    hit = hit.astype(jnp.bfloat16)

    spectrum = jnp.einsum("akc,kn->anc", grid_input, forward, preferred_element_type=jnp.float32)
    spectrum = spectrum.astype(jnp.bfloat16).reshape(lat_dev, 2, orders, channels)
    rows = jnp.einsum("pm,armc->parc", hit, spectrum).astype(jnp.bfloat16)
    rows = rows.reshape(chan_count, group_slots, lat_dev, 2, channels)
    rows = lax.all_to_all(rows, "chan", split_axis=0, concat_axis=0, tiled=True)
    rows = lax.all_gather(rows, "lat", axis=0)
    pairs = lax.all_gather(pairs, "lat", axis=0, tiled=True)

    mixed = jnp.einsum(
        "absurc,bcd->sraud",
        rows,
        mix_weight.reshape(chan_count, channels, -1),
        preferred_element_type=jnp.float32,
    )
    mixed = mixed.reshape(group_slots, 2, latitudes, -1)
    synthesis = jnp.einsum("svt,srtd->vsrd", pairs, mixed, precision=lax.Precision.HIGHEST).astype(jnp.bfloat16)

    synthesis = synthesis.reshape(lat_count, lat_dev, group_slots, 2, -1)
    back = lax.all_to_all(synthesis, "lat", split_axis=0, concat_axis=0, tiled=True)
    back = back.transpose(1, 2, 3, 0, 4).reshape(lat_dev, group_slots, 2, chan_count, channels)
    back = lax.all_to_all(back.transpose(3, 0, 1, 2, 4), "chan", split_axis=0, concat_axis=0, tiled=True)
    back = back.transpose(1, 0, 2, 3, 4).reshape(lat_dev, orders, 2, channels)
    natural = jnp.einsum("pm,aprc->armc", hit, back).astype(jnp.bfloat16)
    field = 2.0 * jnp.einsum(
        "anc,kn->akc",
        natural.reshape(lat_dev, 2 * orders, channels),
        inverse,
        preferred_element_type=jnp.float32,
    )
    return (grid_input.astype(jnp.float32) + jax.nn.gelu(field)).astype(jnp.bfloat16)


def shards(grid_input, legendre, mix_weight, degree_gain, order_slot):
    lat_count, chan_count = lax.axis_size("lat"), lax.axis_size("chan")
    orders, latitudes = order_slot.shape[0], legendre.shape[2]
    compact = (
        lat_count == chan_count == len(STEPS) == len(MEMBERS[0]) // 2
        and 2 * latitudes * latitudes == 128
        and orders % (16 * chan_count) == 0
        and orders <= 256
        and legendre.shape[0] <= PAIR_ROWS
        and grid_input.shape[2] % 128 == 0
        and grid_input.shape[1] % 16 == 0
    )
    body = compact_shards if compact else wide_shards
    return body(grid_input, legendre, mix_weight, degree_gain, order_slot)


def solution(mesh):
    placed = (
        P(("groups", "lat"), None, "chan"),
        P(("lat", "chan"), None, None),
        P(None, "lat"),
        P(),
        P(),
    )
    return jax.shard_map(
        shards,
        mesh=mesh,
        in_specs=placed,
        out_specs=P(("groups", "lat"), None, "chan"),
        check_vma=False,
    )
```
